32 devices in a mesh: ctx: 8 (over z, core), head: 4 (over y, x).
Axes of the slice: x: 2, y: 2, z: 4, core: 2. Of those that a mesh axis runs over, the one named last changes fastest.
Arguments:
- light_query: bfloat16 [4096, 32, 128], P(('ctx', 'head')), may hold values from -6 to 6
- light_keys: bfloat16 [4096, 32, 128], P(('ctx', 'head')), may hold values from -0.5390625 to 0.5390625
- light_values: bfloat16 [4096, 32, 128], P(('ctx', 'head')), may hold values from -6 to 6
- decay_rate: float32 [32], replicated, may hold values from 0.00048828125 to 0.05
- norm_gain: float32 [32, 128], replicated, may hold values from 0.5 to 1.5
- soft_query: bfloat16 [4096, 32, 128], P(('ctx', 'head')), may hold values from -120 to 120
- soft_keys: bfloat16 [4096, 4, 128], P(('ctx', 'head')), may hold values from -8 to 8
- soft_values: bfloat16 [4096, 4, 128], P(('ctx', 'head')), may hold values from -6 to 6
- segment_ids: int32 [4096], P(('ctx', 'head')), may hold values from 0 to 7, never falling along the last dimension, each value on 1 to 1024 neighbouring positions
Outputs:
- light_out: bfloat16 [4096, 32, 128], P(('ctx', 'head'))
- soft_out: bfloat16 [4096, 32, 128], P(('ctx', 'head'))
The draws below stay inside these ranges and needn't reach their ends.
Inputs may be any that keep to these rules, and one draw needn't show every extreme that they name: `segment_ids`: document ids never fall along the tokens; each document covers 1 to 1024 consecutive tokens, and one covers exactly 1024.
All inputs are finite; a program needn't handle non-finite values.
Results may differ from the reference program's by a relative error of at most 0.004.
Values may be sent and summed in bfloat16 or wider, within the bound.
No kernel may reach another device: no remote copies, remote signals or barrier semaphores. Data moves between devices by JAX's collectives and lax.ppermute only.
A program may use at most 64 MiB of HBM per device.

```python
import math
import jax
import jax.numpy as jnp
import numpy as np
from jax import lax

HEADS = 32
HD = 128
KVH = 4
GROUP = 512
TOKENS = 4096
DOC_MOST = 1024
DOCS = 8


def soft_pair(key):
    base = jax.random.fold_in(key, 7001)
    first, second = jax.random.split(base, 2)
    keys_drawn = jnp.clip(jax.random.normal(first, (TOKENS, KVH, HD), jnp.float32), -6.0, 6.0)
    query_drawn = jnp.clip(jax.random.normal(second, (TOKENS, HEADS, HD), jnp.float32), -6.0, 6.0)
    return (query_drawn, keys_drawn)


def draw_soft_query(key, part):
    return soft_pair(key)[0].astype(jnp.bfloat16)


def draw_soft_keys(key, part):
    return soft_pair(key)[1].astype(jnp.bfloat16)


def levels(stream_key, extent, shards, least, top_value):
    loudness, own = 1.0, jax.random.fold_in(stream_key, 6)
    for axis_at, shards_of in shards:
        draws = jnp.exp(jax.random.uniform(jax.random.fold_in(own, axis_at), (shards_of,), jnp.float32, least / len(shards), top_value / len(shards)))
        loudness = loudness * jnp.repeat(draws, extent[axis_at] // shards_of).reshape([-1 if axis == axis_at else 1 for axis in range(len(extent))])
    return loudness


def split_up(number_of, total, most, skew):
    weights = [(1 << 20) // math.isqrt(standing ** skew) + 1 for standing in range(2, number_of + 1)]
    surplus, given = total - most - (number_of - 1), [1] * (number_of - 1)
    while surplus > 0:
        free = [i for i in range(number_of - 1) if given[i] < most]
        whole, remaining = sum([weights[i] for i in free]), surplus
        for i in free:
            more = min(most - given[i], max(1, remaining * weights[i] // whole), surplus)
            given[i] = given[i] + more
            surplus = surplus - more
    return np.array([most] + given)


def uneven_parts(key, amount, total, bound, slope):
    if amount == 2:
        one = jax.random.randint(key, (), max(1, total - bound), min(bound, total - 1) + 1)
        return jnp.stack([one, total - one])
    sizes = jnp.asarray(split_up(amount, total, bound, slope), jnp.int32)
    couples = (amount - 1) // 2
    source_of, sink = sizes[1:1 + 2 * couples:2], sizes[2:2 + 2 * couples:2]
    slack = jnp.minimum(source_of - 1, bound - sink)
    passed = jax.random.randint(jax.random.fold_in(key, 1), (couples,), 0, 1 << 20) % (slack + 1)
    sizes = sizes.at[1:1 + 2 * couples:2].set(source_of - passed).at[2:2 + 2 * couples:2].set(sink + passed)
    return sizes[jax.random.permutation(jax.random.fold_in(key, 2), amount)]


def normal_values(rng, extent, width, most, cuts=(), held_as=jnp.bfloat16):
    drawn = width * jax.random.normal(rng, extent, jnp.float32)
    if cuts:
        drawn = drawn * levels(rng, extent, cuts, -0.22, 0.18)
    return jnp.clip(drawn, -most, most).astype(held_as)


def setup_inputs(seed: int = 0) -> dict:
    keys = jax.random.split(jax.random.key(seed), 10)
    light_query = normal_values(keys[0], (TOKENS, HEADS, HD), 1.0, 6.0, ((0, 32),))
    light_keys = normal_values(keys[1], (TOKENS, HEADS, HD), 0.09, 0.5390625, ((0, 32),))
    light_values = normal_values(keys[2], (TOKENS, HEADS, HD), 1.0, 6.0, ((0, 32),))
    decay_rate = jnp.clip(jnp.exp(jax.random.uniform(keys[3], (HEADS,), jnp.float32, math.log(0.00048828125), math.log(0.05))), 0.00048828125, 0.05)
    norm_gain = jnp.clip(1.0 + 0.1 * jax.random.normal(keys[4], (HEADS, HD), jnp.float32), 0.5, 1.5)
    soft_query = draw_soft_query(jax.random.fold_in(keys[9], 71), 0)
    soft_keys = draw_soft_keys(jax.random.fold_in(keys[9], 71), 0)
    soft_values = normal_values(keys[7], (TOKENS, KVH, HD), 1.0, 6.0, ((0, 32),))
    segment_ids = jnp.searchsorted(jnp.cumsum(uneven_parts(keys[8], DOCS, TOKENS, DOC_MOST, 2)), jnp.arange(TOKENS), side="right").astype(jnp.int32)
    return {"light_query": light_query, "light_keys": light_keys, "light_values": light_values, "decay_rate": decay_rate, "norm_gain": norm_gain, "soft_query": soft_query, "soft_keys": soft_keys, "soft_values": soft_values, "segment_ids": segment_ids}


HIGH = lax.Precision.HIGHEST
NEG_FILL = -1e+30
NORM_EPS = 1e-06

def lightning_core(light_query, light_keys, light_values, decay_rate, segment_ids):
    block = min(512, GROUP)
    blocks = TOKENS // block
    query_blocks = light_query.reshape(blocks, block, HEADS, HD)
    key_blocks = light_keys.reshape(blocks, block, HEADS, HD)
    value_blocks = light_values.reshape(blocks, block, HEADS, HD)
    sid_blocks = segment_ids.reshape(blocks, block)
    offsets = jnp.arange(block, dtype=jnp.int32)
    distance = offsets[:, None] - offsets[None, :]
    causal = distance >= 0
    spread = jnp.maximum(distance, 0).astype(jnp.float32)
    within = jnp.exp(-decay_rate[:, None, None] * spread[None])
    lead_decay = jnp.exp(-decay_rate[None, :] * (offsets + 1).astype(jnp.float32)[:, None])
    tail_decay = jnp.exp(-decay_rate[None, :] * (block - 1 - offsets).astype(jnp.float32)[:, None])
    full_decay = jnp.exp(-decay_rate * block)

    def advance(carried, inputs):
        state_now, prev_sid = carried
        query_block, key_block, value_block, sid_block = inputs
        query_wide = query_block.astype(jnp.float32)
        key_wide = key_block.astype(jnp.float32)
        value_wide = value_block.astype(jnp.float32)
        allowed = causal & (sid_block[:, None] == sid_block[None, :])
        scores = jnp.einsum('thd,jhd->htj', query_wide, key_wide, precision=HIGH)
        weights = scores * jnp.where(allowed[None], within, 0.0)
        local_part = jnp.einsum('htj,jhd->thd', weights, value_wide, precision=HIGH)
        carry_in = (sid_block == prev_sid).astype(jnp.float32)
        inherited = jnp.einsum('thd,hde->the', query_wide, state_now, precision=HIGH)
        inherited = inherited * (lead_decay * carry_in[:, None])[:, :, None]
        last_sid = sid_block[-1]
        keep_rate = jnp.where(last_sid == prev_sid, full_decay, 0.0)
        open_doc = (sid_block == last_sid).astype(jnp.float32)
        weighted_keys = key_wide * (tail_decay * open_doc[:, None])[:, :, None]
        state_next = keep_rate[:, None, None] * state_now + jnp.einsum('jhd,jhe->hde', weighted_keys, value_wide, precision=HIGH)
        return ((state_next, last_sid), local_part + inherited)
    initial = (jnp.zeros((HEADS, HD, HD), jnp.float32), jnp.int32(-1))
    _, outputs = lax.scan(advance, initial, (query_blocks, key_blocks, value_blocks, sid_blocks))
    return outputs.reshape(TOKENS, HEADS, HD)

def softmax_core(soft_query, soft_keys, soft_values, segment_ids):
    tile = min(512, GROUP)
    share = HEADS // KVH
    scale = HD ** (-0.5)
    reach = DOC_MOST
    padded_keys = jnp.concatenate([jnp.zeros((reach, KVH, HD), soft_keys.dtype), soft_keys], 0)
    padded_values = jnp.concatenate([jnp.zeros((reach, KVH, HD), soft_values.dtype), soft_values], 0)
    padded_sids = jnp.concatenate([-jnp.ones((reach,), jnp.int32), segment_ids.astype(jnp.int32)], 0)

    def attend(tile_index):
        start = (tile_index * tile).astype(jnp.int32)
        query_tile = lax.dynamic_slice_in_dim(soft_query, start, tile, 0).astype(jnp.float32).reshape(tile, KVH, share, HD)
        key_tile = lax.dynamic_slice_in_dim(padded_keys, start, reach + tile, 0).astype(jnp.float32)
        value_tile = lax.dynamic_slice_in_dim(padded_values, start, reach + tile, 0).astype(jnp.float32)
        query_sid = lax.dynamic_slice_in_dim(segment_ids.astype(jnp.int32), start, tile, 0)
        key_sid = lax.dynamic_slice_in_dim(padded_sids, start, reach + tile, 0)
        query_pos = start + jnp.arange(tile, dtype=jnp.int32)
        key_pos = start - reach + jnp.arange(reach + tile, dtype=jnp.int32)
        allowed = (key_pos[None, :] <= query_pos[:, None]) & (key_sid[None, :] == query_sid[:, None])
        scores = jnp.einsum('tkgd,jkd->kgtj', query_tile, key_tile, precision=HIGH) * scale
        scores = jnp.where(allowed[None, None], scores, NEG_FILL)
        peak = lax.optimization_barrier(jnp.max(scores, axis=-1, keepdims=True))
        probs = jnp.exp(scores - peak)
        total = lax.optimization_barrier(jnp.sum(probs, axis=-1))
        rounded = lax.optimization_barrier(probs.astype(jnp.bfloat16))
        mixed = jnp.einsum('kgtj,jkd->kgtd', rounded.astype(jnp.float32), value_tile, precision=HIGH)
        mixed = mixed / total[..., None]
        return jnp.transpose(mixed, (2, 0, 1, 3)).reshape(tile, HEADS, HD).astype(jnp.bfloat16)
    tiles = lax.map(attend, jnp.arange(TOKENS // tile, dtype=jnp.int32))
    return tiles.reshape(TOKENS, HEADS, HD)

def reference(light_query, light_keys, light_values, decay_rate, norm_gain, soft_query, soft_keys, soft_values, segment_ids):
    light_raw = lightning_core(light_query, light_keys, light_values, decay_rate, segment_ids)
    mean_square = lax.optimization_barrier(jnp.mean(light_raw * light_raw, axis=-1, keepdims=True))
    light_out = (light_raw * lax.rsqrt(mean_square + NORM_EPS) * norm_gain[None]).astype(jnp.bfloat16)
    soft_out = softmax_core(soft_query, soft_keys, soft_values, segment_ids)
    return (light_out, soft_out)
```

```python
import functools
import math

import jax
import jax.numpy as jnp
from jax import lax
from jax.experimental import pallas as pl
from jax.experimental.pallas import tpu as pltpu
from jax.sharding import PartitionSpec as P

LOOK = 2
NEG_FILL = -1e30
NORM_EPS = 1e-06
TAIL = 16
F32 = jnp.float32
BF16 = jnp.bfloat16
AXES = ("ctx", "head")


def params(limit_mib):
    return pltpu.CompilerParams(vmem_limit_bytes=limit_mib * 1024 * 1024)


def vmem_specs(count):
    return [pl.BlockSpec(memory_space=pltpu.VMEM)] * count


def smem_specs(count):
    return [pl.BlockSpec(memory_space=pltpu.SMEM)] * count


def column(row):
    size = row.shape[1]
    return jnp.transpose(jnp.broadcast_to(row, (size, size)))


def dot(left, right, contract):
    return lax.dot_general(left, right, (contract, ((), ())), preferred_element_type=F32)


def split(value):
    high = value.astype(BF16)
    return high, (value - high.astype(F32)).astype(BF16)


def source_kernel(members, me_ref, rate_ref, sid_ref, key_ref, value_ref, skey_ref, svalue_ref, *rest):
    outs, pay_ref = rest[:members], rest[members]
    key_wide, value_wide, small = rest[members + 1 :]
    tokens, heads, width = key_ref.shape
    kv_heads = skey_ref.shape[1]
    per = heads // members
    me = me_ref[0]
    sid_row = (sid_ref[...] + 1).astype(F32)
    tail = jnp.broadcast_to(sid_row, (TAIL, tokens)).astype(BF16)
    open_row = (sid_row == jnp.max(sid_row, axis=1, keepdims=True)).astype(F32)
    open_column = column(open_row)
    behind = (tokens - 1 - lax.broadcasted_iota(jnp.int32, (tokens, width), 0)).astype(F32)
    for at, ref in enumerate((skey_ref, svalue_ref)):
        small[...] = ref[...].astype(F32).reshape(tokens * kv_heads, width)
        for g in range(kv_heads):
            rows = pl.ds((at * kv_heads + g) * tokens, tokens)
            pay_ref[rows, :] = small[pl.ds(g, tokens, stride=kv_heads), :].astype(BF16)
    pay_ref[pl.ds(2 * kv_heads * tokens, TAIL), :] = tail
    key_wide[...] = key_ref[...].astype(F32).reshape(tokens * heads, width)
    value_wide[...] = value_ref[...].astype(F32).reshape(tokens * heads, width)
    for k in range(members):
        for j in range(per):
            head = (me ^ k) * per + j
            keys = key_wide[pl.ds(head, tokens, stride=heads), :]
            values = value_wide[pl.ds(head, tokens, stride=heads), :].astype(BF16)
            weighted = keys * (open_column * jnp.exp(-rate_ref[head] * behind))
            high, low = split(weighted)
            state = dot(
                jnp.concatenate([high, low], 0), jnp.concatenate([values, values], 0), ((0,), (0,))
            )
            outs[k][pl.ds(j * width, width), :] = state.astype(BF16)
        outs[k][pl.ds(per * width, TAIL), :] = tail


def gather_slots(members, me, pays, slots):
    for k in range(members):
        slots[me ^ k] = pays[k][...]


def advance(slots, block, per, width, tokens, rates, state, last):
    tail = slots[block, pl.ds(per * width, TAIL), :].astype(F32)
    now = jnp.max(tail, axis=(0, 1), keepdims=True)
    same = (now == last).astype(F32)
    state = [
        slots[block, pl.ds(j * width, width), :].astype(F32)
        + (same * jnp.exp(jnp.full((1, width), -rates[j] * tokens, F32))) * state[j]
        for j in range(per)
    ]
    return state, now


def ending_kernel(members, tokens, me_ref, rate_ref, *rest):
    pays, out_ref, slots = rest[:members], rest[members], rest[members + 1]
    width = out_ref.shape[1]
    per = (out_ref.shape[0] - TAIL) // width
    me = me_ref[0]
    gather_slots(members, me, pays, slots)
    rates = [rate_ref[me * per + j] for j in range(per)]
    state = [jnp.zeros((width, width), F32)] * per
    last = jnp.zeros((1, 1), F32)
    for block in range(members):
        state, last = advance(slots, block, per, width, tokens, rates, state, last)
    for j in range(per):
        out_ref[pl.ds(j * width, width), :] = state[j].astype(BF16)
    out_ref[pl.ds(per * width, TAIL), :] = jnp.broadcast_to(last, (TAIL, width)).astype(BF16)


def prefix_kernel(members, tokens, me_ref, rate_ref, entry_ref, *rest):
    pays, outs = rest[:members], rest[members : 2 * members]
    slots, results = rest[2 * members :]
    width = entry_ref.shape[1]
    per = (entry_ref.shape[0] - TAIL) // width
    me = me_ref[0]
    gather_slots(members, me, pays, slots)
    rates = [rate_ref[me * per + j] for j in range(per)]
    state = [entry_ref[pl.ds(j * width, width), :].astype(F32) for j in range(per)]
    last = jnp.max(entry_ref[pl.ds(per * width, TAIL), :].astype(F32), axis=(0, 1), keepdims=True)
    for block in range(members):
        for j in range(per):
            results[block, pl.ds(j * width, width), :] = state[j].astype(BF16)
        results[block, pl.ds(per * width, TAIL), :] = jnp.broadcast_to(last, (TAIL, width)).astype(BF16)
        if block < members - 1:
            state, last = advance(slots, block, per, width, tokens, rates, state, last)
    for k in range(members):
        outs[k][...] = results[me ^ k]


def light_kernel(members, me_ref, rate_ref, sid_ref, gain_ref, query_ref, key_ref, value_ref, *rest):
    pays, out_ref = rest[:members], rest[members]
    query_wide, key_wide, value_wide, out_wide = rest[members + 1 :]
    tokens, heads, width = query_ref.shape
    per = heads // members
    me = me_ref[0]
    sid_row = (sid_ref[...] + 1).astype(F32)
    sid_column = column(sid_row)
    entry = jnp.max(pays[0][pl.ds(per * width, TAIL), :].astype(F32), axis=(0, 1), keepdims=True)
    continues = (sid_column == entry).astype(F32)
    row_at = lax.broadcasted_iota(jnp.int32, (tokens, tokens), 0)
    distance = row_at - lax.broadcasted_iota(jnp.int32, (tokens, tokens), 1)
    allowed = ((distance >= 0) & (sid_column == sid_row)).astype(F32)
    spread = jnp.maximum(distance, 0).astype(F32)
    ahead = (row_at + 1).astype(F32)
    query_wide[...] = query_ref[...].astype(F32).reshape(tokens * heads, width)
    key_wide[...] = key_ref[...].astype(F32).reshape(tokens * heads, width)
    value_wide[...] = value_ref[...].astype(F32).reshape(tokens * heads, width)
    for k in range(members):
        for j in range(per):
            head = (me ^ k) * per + j
            rows = pl.ds(head, tokens, stride=heads)
            query = query_wide[rows, :].astype(BF16)
            keys = key_wide[rows, :].astype(BF16)
            values = value_wide[rows, :].astype(BF16)
            rate = rate_ref[head]
            weights = dot(query, keys, ((1,), (1,))) * (allowed * jnp.exp(-rate * spread))
            high, low = split(weights)
            raw = dot(
                jnp.concatenate([high, low], 1), jnp.concatenate([values, values], 0), ((1,), (0,))
            )
            inherited = dot(query, pays[k][pl.ds(j * width, width), :], ((1,), (0,)))
            raw = raw + inherited * (continues * jnp.exp(-rate * ahead))
            mean_square = jnp.mean(raw * raw, axis=1, keepdims=True)
            gain = gain_ref[pl.ds(head, 1), :]
            out_wide[rows, :] = raw * lax.rsqrt(mean_square + NORM_EPS) * gain
    out_ref[...] = out_wide[...].reshape(tokens, heads, width).astype(BF16)


def soft_kernel(blocks, kv_heads, chunk, sid_ref, query_ref, *rest):
    pays, out_ref = rest[:blocks], rest[blocks]
    keys_all, values_all, bias = rest[blocks + 1 :]
    tokens, heads, width = query_ref.shape
    share = heads // kv_heads
    sid_row = (sid_ref[...] + 1).astype(F32)
    sid_column = column(sid_row)
    causal = lax.broadcasted_iota(jnp.int32, (tokens, tokens), 0) >= lax.broadcasted_iota(
        jnp.int32, (tokens, tokens), 1
    )
    for at in range(blocks):
        span = pl.ds(at * tokens, tokens)
        for g in range(kv_heads):
            keys_all[g, span, :] = pays[at][pl.ds(g * tokens, tokens), :]
            values_all[g, span, :] = pays[at][pl.ds((kv_heads + g) * tokens, tokens), :]
        key_sid = pays[at][pl.ds(2 * kv_heads * tokens, TAIL), :].astype(F32)[0:1, :]
        allowed = sid_column == key_sid
        if at == blocks - 1:
            allowed = allowed & causal
        fill = jnp.where(allowed, 0.0, NEG_FILL).reshape(tokens, 1, tokens)
        bias[:, span] = jnp.broadcast_to(fill, (tokens, share, tokens)).reshape(tokens * share, tokens)
    factor = width ** (-0.5) * math.log2(math.e)
    pair = 2

    def step(at, carry):
        start = pl.multiple_of(at * chunk, chunk)
        rows = pl.ds(pl.multiple_of(at * chunk * share, chunk * share), chunk * share)
        for gg in range(kv_heads // pair):
            query_wide = query_ref[pl.ds(start, chunk), pl.ds(gg * pair * share, pair * share), :].astype(F32)
            mixed = []
            for s in range(pair):
                g = gg * pair + s
                query = query_wide[:, s * share : (s + 1) * share, :].reshape(chunk * share, width).astype(BF16)
                scores = dot(query, keys_all[g], ((1,), (1,))) + bias[rows, :]
                peak = jnp.max(scores, axis=1, keepdims=True)
                probs = jnp.exp2((scores - peak) * factor)
                total = jnp.sum(probs, axis=1, keepdims=True)
                out = dot(probs.astype(BF16), values_all[g], ((1,), (0,))) / total
                mixed.append(out.reshape(chunk, share, width))
            out_ref[pl.ds(start, chunk), pl.ds(gg * pair * share, pair * share), :] = jnp.concatenate(
                mixed, 1
            ).astype(BF16)
        return carry

    lax.fori_loop(0, tokens // chunk, step, 0)


def body(
    light_query,
    light_keys,
    light_values,
    decay_rate,
    norm_gain,
    soft_query,
    soft_keys,
    soft_values,
    segment_ids,
):
    n_head = lax.axis_size("head")
    n_all = lax.axis_size("ctx") * n_head
    members = LOOK * n_head
    me = lax.rem(lax.axis_index("ctx"), LOOK) * n_head + lax.axis_index("head")
    me_arg = jnp.reshape(me, (1,)).astype(jnp.int32)
    tokens, heads, width = light_query.shape
    kv_heads = soft_keys.shape[1]
    per = heads // members
    sid_row = segment_ids.reshape(1, tokens)

    def partner(value, k):
        pairs = [(i, i - i % members + ((i % members) ^ k)) for i in range(n_all)]
        return lax.ppermute(value, AXES, pairs)

    def onward(value):
        return lax.ppermute(value, AXES, [(i, i + members) for i in range(n_all - members)])

    state_shape = jax.ShapeDtypeStruct((per * width + TAIL, width), BF16)
    pay_shape = jax.ShapeDtypeStruct((2 * kv_heads * tokens + TAIL, width), BF16)
    wide = pltpu.VMEM((tokens * heads, width), F32)
    slots = pltpu.VMEM((members,) + state_shape.shape, BF16)

    made = pl.pallas_call(
        functools.partial(source_kernel, members),
        out_shape=[state_shape] * members + [pay_shape],
        in_specs=smem_specs(2) + vmem_specs(5),
        out_specs=vmem_specs(members + 1),
        scratch_shapes=[wide, wide, pltpu.VMEM((tokens * kv_heads, width), F32)],
        compiler_params=params(32),
        name="source",
    )(me_arg, decay_rate, sid_row, light_keys, light_values, soft_keys, soft_values)
    states, own_pay = made[:members], made[members]

    prev_pay = onward(own_pay)
    states = [states[0]] + [partner(states[k], k) for k in range(1, members)]
    ending = pl.pallas_call(
        functools.partial(ending_kernel, members, tokens),
        out_shape=state_shape,
        in_specs=smem_specs(2) + vmem_specs(members),
        out_specs=vmem_specs(1)[0],
        scratch_shapes=[slots],
        compiler_params=params(32),
        name="ending",
    )(me_arg, decay_rate, *states)
    entry = onward(ending)
    window = [prev_pay]
    for k in range(1, members):
        later = (me ^ k) > me
        window.append(partner(jnp.where(later, own_pay, prev_pay), k))
    window.append(own_pay)
    entries = pl.pallas_call(
        functools.partial(prefix_kernel, members, tokens),
        out_shape=[state_shape] * members,
        in_specs=smem_specs(2) + vmem_specs(members + 1),
        out_specs=vmem_specs(members),
        scratch_shapes=[slots, slots],
        compiler_params=params(32),
        name="prefix",
    )(me_arg, decay_rate, entry, *states)
    entries = [entries[0]] + [partner(entries[k], k) for k in range(1, members)]

    blocks = members + 1
    chunk = math.gcd(tokens, 32)
    soft_out = pl.pallas_call(
        functools.partial(soft_kernel, blocks, kv_heads, chunk),
        out_shape=jax.ShapeDtypeStruct((tokens, heads, width), BF16),
        in_specs=vmem_specs(2 + blocks),
        out_specs=vmem_specs(1)[0],
        scratch_shapes=[
            pltpu.VMEM((kv_heads, blocks * tokens, width), BF16),
            pltpu.VMEM((kv_heads, blocks * tokens, width), BF16),
            pltpu.VMEM((tokens * heads // kv_heads, blocks * tokens), F32),
        ],
        compiler_params=params(60),
        cost_estimate=pl.CostEstimate(
            flops=4 * tokens * heads * blocks * tokens * width,
            bytes_accessed=4 * tokens * heads * width + blocks * 4 * kv_heads * tokens * width,
            transcendentals=tokens * heads * blocks * tokens,
        ),
        name="soft",
    )(sid_row, soft_query, *window)

    light_out = pl.pallas_call(
        functools.partial(light_kernel, members),
        out_shape=jax.ShapeDtypeStruct((tokens, heads, width), BF16),
        in_specs=smem_specs(2) + vmem_specs(5 + members),
        out_specs=vmem_specs(1)[0],
        scratch_shapes=[wide] * 4,
        compiler_params=params(48),
        name="light",
    )(me_arg, decay_rate, sid_row, norm_gain, light_query, light_keys, light_values, *entries)
    return (light_out, soft_out)


def solution(mesh):
    placed = P(("ctx", "head"), None, None)
    return jax.shard_map(
        body,
        mesh=mesh,
        in_specs=(placed, placed, placed, P(), P(), placed, placed, placed, P(("ctx", "head"))),
        out_specs=(placed, placed),
        check_vma=False,
    )
```

```python
import functools
import math

import jax
import jax.numpy as jnp
from jax import lax
from jax.experimental import pallas as pl
from jax.experimental.pallas import tpu as pltpu
from jax.sharding import PartitionSpec as P

LOOK = 2
NEG_FILL = -1e30
NORM_EPS = 1e-06
TAIL = 16
F32 = jnp.float32
BF16 = jnp.bfloat16
AXES = ("ctx", "head")
VMEM = pl.BlockSpec(memory_space=pltpu.VMEM)
SMEM = pl.BlockSpec(memory_space=pltpu.SMEM)
ANY = pl.BlockSpec(memory_space=pl.ANY)


def call(kernel, name, micros, limit_mib, ins, outs, out_specs, scratch=()):
    return pl.pallas_call(
        kernel,
        out_shape=outs,
        in_specs=ins,
        out_specs=out_specs,
        scratch_shapes=list(scratch),
        compiler_params=pltpu.CompilerParams(vmem_limit_bytes=int(limit_mib * 1024 * 1024)),
        cost_estimate=pl.CostEstimate(flops=int(micros * 1e9), bytes_accessed=0, transcendentals=0),
        name=name,
    )


def column(row):
    size = row.shape[1]
    return jnp.transpose(jnp.broadcast_to(row, (size, size)))


def dot(left, right, contract):
    return lax.dot_general(left, right, (contract, ((), ())), preferred_element_type=F32)


def split(value):
    high = value.astype(BF16)
    return high, (value - high.astype(F32)).astype(BF16)


def pack_kernel(at_ref, sid_ref, key_ref, value_ref, query_ref, keep_ref, give_ref, query_give, key_in, value_in, stage, sems):
    tokens, kv_heads, width = key_in.shape
    half, heads = kv_heads // LOOK, query_ref.shape[1] // LOOK
    core = at_ref[0]
    other = LOOK - 1 - core
    copies = [
        pltpu.make_async_copy(key_ref, key_in, sems.at[0]),
        pltpu.make_async_copy(value_ref, value_in, sems.at[1]),
        pltpu.make_async_copy(
            query_ref.at[:, pl.ds(pl.multiple_of(other * heads, heads), heads), :], query_give, sems.at[2]
        ),
    ]
    for copy in copies:
        copy.start()
    tail = jnp.broadcast_to((sid_ref[...] + 1).astype(F32), (TAIL, tokens)).astype(BF16)
    for at, ref in enumerate((key_in, value_in)):
        copies[at].wait()
        stage[...] = jnp.swapaxes(ref[...], 0, 1)
        for j in range(half):
            rows = pl.ds((at * half + j) * tokens, tokens)
            keep_ref[rows, :] = stage[core * half + j]
            give_ref[rows, :] = stage[other * half + j]
    keep_ref[pl.ds(2 * half * tokens, TAIL), :] = tail
    give_ref[pl.ds(2 * half * tokens, TAIL), :] = tail
    copies[2].wait()


def mix_kernel(places, at_ref, mine, theirs, mine_before, theirs_before, home_ref, *outs):
    core, place = at_ref[0], at_ref[1]
    home_ref[2 * core] = mine[...]
    home_ref[2 * (1 - core)] = theirs[...]
    home_ref[2 * core + 1] = mine_before[...]
    home_ref[2 * (1 - core) + 1] = theirs_before[...]
    for k in range(1, places):
        out = outs[k - 1]
        later = ((place ^ k) > place).astype(jnp.int32)
        out[0] = home_ref[0]
        out[1] = home_ref[3]
        out[2] = home_ref[1 + later]


def source_kernel(members, at_ref, rate_ref, sid_ref, key_ref, value_ref, *rest):
    outs, keys_by_head, values_by_head = rest[:members], rest[members], rest[members + 1]
    key_in, value_in, sems = rest[members + 2 :]
    heads, tokens, width = keys_by_head.shape
    per = heads // members
    me = at_ref[2]
    copies = [
        pltpu.make_async_copy(key_ref, key_in, sems.at[0]),
        pltpu.make_async_copy(value_ref, value_in, sems.at[1]),
    ]
    for copy in copies:
        copy.start()
    sid_row = (sid_ref[...] + 1).astype(F32)
    tail = jnp.broadcast_to(sid_row, (TAIL, tokens)).astype(BF16)
    open_row = (sid_row == jnp.max(sid_row, axis=1, keepdims=True)).astype(F32)
    behind = (tokens - 1 - lax.broadcasted_iota(jnp.int32, (1, tokens), 1)).astype(F32)
    copies[0].wait()
    keys_by_head[...] = jnp.swapaxes(key_in[...], 0, 1)
    copies[1].wait()
    values_by_head[...] = jnp.swapaxes(value_in[...], 0, 1)
    for k in range(members):
        for j in range(per):
            head = (me ^ k) * per + j
            values = values_by_head[head]
            weighted = jnp.transpose(keys_by_head[head].astype(F32)) * (open_row * jnp.exp(-rate_ref[head] * behind))
            high, low = split(weighted)
            state = dot(jnp.concatenate([high, low], 1), jnp.concatenate([values, values], 0), ((1,), (0,)))
            outs[k][pl.ds(j * width, width), :] = state.astype(BF16)
        outs[k][pl.ds(per * width, TAIL), :] = tail


def gather_slots(members, me, pays, slots):
    for k in range(members):
        slots[me ^ k] = pays[k][...]


def advance(slots, block, per, width, tokens, rates, state, last):
    tail = slots[block, pl.ds(per * width, TAIL), :].astype(F32)
    now = jnp.max(tail, axis=(0, 1), keepdims=True)
    same = (now == last).astype(F32)
    state = [
        slots[block, pl.ds(j * width, width), :].astype(F32)
        + (same * jnp.exp(jnp.full((1, width), -rates[j] * tokens, F32))) * state[j]
        for j in range(per)
    ]
    return state, now


def ending_kernel(members, tokens, at_ref, rate_ref, *rest):
    pays, out_ref, slots = rest[:members], rest[members], rest[members + 1]
    width = out_ref.shape[1]
    per = (out_ref.shape[0] - TAIL) // width
    me = at_ref[2]
    gather_slots(members, me, pays, slots)
    rates = [rate_ref[me * per + j] for j in range(per)]
    state = [jnp.zeros((width, width), F32)] * per
    last = jnp.zeros((1, 1), F32)
    for block in range(members):
        state, last = advance(slots, block, per, width, tokens, rates, state, last)
    for j in range(per):
        out_ref[pl.ds(j * width, width), :] = state[j].astype(BF16)
    out_ref[pl.ds(per * width, TAIL), :] = jnp.broadcast_to(last, (TAIL, width)).astype(BF16)


def prefix_kernel(members, tokens, at_ref, rate_ref, entry_ref, *rest):
    pays, outs = rest[:members], rest[members : 2 * members]
    slots, results = rest[2 * members :]
    width = entry_ref.shape[1]
    per = (entry_ref.shape[0] - TAIL) // width
    me = at_ref[2]
    gather_slots(members, me, pays, slots)
    rates = [rate_ref[me * per + j] for j in range(per)]
    state = [entry_ref[pl.ds(j * width, width), :].astype(F32) for j in range(per)]
    last = jnp.max(entry_ref[pl.ds(per * width, TAIL), :].astype(F32), axis=(0, 1), keepdims=True)
    for block in range(members):
        for j in range(per):
            results[block, pl.ds(j * width, width), :] = state[j].astype(BF16)
        results[block, pl.ds(per * width, TAIL), :] = jnp.broadcast_to(last, (TAIL, width)).astype(BF16)
        if block < members - 1:
            state, last = advance(slots, block, per, width, tokens, rates, state, last)
    for k in range(members):
        outs[k][...] = results[me ^ k]


def prep_kernel(rate_ref, sid_ref, query_ref, keys_by_head, left_ref):
    heads, tokens, _ = keys_by_head.shape
    sid_row = (sid_ref[...] + 1).astype(F32)
    row_at = lax.broadcasted_iota(jnp.int32, (tokens, tokens), 0)
    lane = lax.broadcasted_iota(jnp.int32, (tokens, tokens), 1)
    allowed = ((row_at >= lane) & (column(sid_row) == sid_row)).astype(F32)
    ahead = (lax.broadcasted_iota(jnp.int32, (1, tokens), 1) + 1).astype(F32)
    left_ref[:, :, tokens:] = jnp.swapaxes(query_ref[...], 0, 1)
    for head in range(heads):
        weights = dot(left_ref[head, :, tokens:], keys_by_head[head], ((1,), (1,)))
        weights = weights * allowed * jnp.exp(rate_ref[head] * ahead)
        left_ref[head, :, :tokens] = weights.astype(BF16)


def final_kernel(members, at_ref, rate_ref, sid_ref, gain_ref, left_ref, values_by_head, keep_ref, got_ref, *rest):
    pays, light_ref, soft_ref, by_head = rest[:members], rest[members], rest[members + 1], rest[members + 2]
    tokens, heads, width = light_ref.shape
    per, half = heads // members, heads // LOOK
    core, me = at_ref[0], at_ref[2]
    soft_ref[:, pl.ds(pl.multiple_of(core * half, half), half), :] = keep_ref[...]
    soft_ref[:, pl.ds(pl.multiple_of((1 - core) * half, half), half), :] = got_ref[...]
    sid_column = column((sid_ref[...] + 1).astype(F32))
    entry = jnp.max(pays[0][pl.ds(per * width, TAIL), :].astype(F32), axis=(0, 1), keepdims=True)
    continues = (sid_column == entry).astype(BF16)
    ahead = (lax.broadcasted_iota(jnp.int32, (tokens, 1), 0) + 1).astype(F32)
    for k in range(members):
        for j in range(per):
            head = (me ^ k) * per + j
            left = jnp.concatenate([left_ref[head, :, :tokens], left_ref[head, :, tokens:] * continues], 1)
            right = jnp.concatenate([values_by_head[head], pays[k][pl.ds(j * width, width), :]], 0)
            raw = dot(left, right, ((1,), (0,)))
            lead = jnp.exp(-rate_ref[head] * ahead)
            mean_square = jnp.mean(raw * raw, axis=1, keepdims=True) * (lead * lead)
            out = raw * (lead * lax.rsqrt(mean_square + NORM_EPS)) * gain_ref[pl.ds(head, 1), :]
            by_head[head] = out.astype(BF16)
    light_ref[...] = jnp.swapaxes(by_head[...], 0, 1)


def soft_kernel(places, chunk, own, at_ref, query_ref, home_ref, *rest):
    pays, out_ref = rest[: places - 1], rest[places - 1]
    marks, codes, fills = rest[places:]
    tokens, heads, width = out_ref.shape
    kv_heads = (home_ref.shape[1] - TAIL) // (2 * tokens)
    share = heads // kv_heads
    core, place = at_ref[0], at_ref[1]
    block = core if own else 1 - core
    first_head = pl.multiple_of(core * heads, heads) if own else 0
    picks = [(home_ref, 1 - block), (home_ref, 3)]
    for k in range(1, places):
        later = ((place ^ k) > place).astype(jnp.int32)
        picks.append((pays[k - 1], 2 * later * (1 - block)))
        picks.append((pays[k - 1], 1 + (1 - later) * block))
    picks.append((home_ref, 2 * block))
    blocks = len(picks)
    lane = lax.broadcasted_iota(jnp.int32, (tokens, tokens), 1)
    lane_wide = lane.astype(F32)

    def spread(value):
        value = jnp.broadcast_to(value.reshape(tokens, 1, tokens), (tokens, share, tokens))
        return value.reshape(tokens * share, tokens)

    for at, (ref, slot) in enumerate(picks):
        sids = column(ref[slot, pl.ds(2 * kv_heads * tokens, TAIL), :].astype(F32)[0:1, :])
        codes[pl.ds(at * tokens, tokens), :] = (sids == lane_wide).astype(BF16)
        if at == blocks - 1:
            marks[...] = spread(jnp.where(sids == lane_wide, 0.0, NEG_FILL)).astype(BF16)
    row_at = lax.broadcasted_iota(jnp.int32, (tokens, tokens), 0)
    fills[...] = spread(jnp.where(row_at >= lane, 0.0, NEG_FILL))
    factor = width ** (-0.5) * math.log2(math.e)
    last = (blocks - 1) * tokens
    ones = jnp.ones((blocks * tokens, width), BF16)

    def step(at, carry):
        start = at * chunk
        rows = pl.ds(start * share, chunk * share)
        query_wide = query_ref[pl.ds(start, chunk), pl.ds(first_head, heads), :].astype(F32)
        mixed = []
        for g in range(kv_heads):
            query = query_wide[:, g * share : (g + 1) * share, :].reshape(chunk * share, width).astype(BF16)
            query = jnp.concatenate([query, marks[rows, :]], 1)
            keys = jnp.concatenate([ref[slot, pl.ds(g * tokens, tokens), :] for ref, slot in picks], 0)
            scores = dot(query, jnp.concatenate([keys, codes[...]], 1), ((1,), (1,)))
            scores = jnp.concatenate([scores[:, :last], scores[:, last:] + fills[rows, :]], 1)
            peak = jnp.max(scores, axis=1, keepdims=True)
            probs = jnp.exp2((scores - peak) * factor).astype(BF16)
            values = jnp.concatenate([ref[slot, pl.ds((kv_heads + g) * tokens, tokens), :] for ref, slot in picks], 0)
            out = dot(probs, jnp.concatenate([values, ones], 1), ((1,), (0,)))
            mixed.append((out[:, :width] / out[:, width:]).reshape(chunk, share, width))
        out_ref[pl.ds(start, chunk), :, :] = jnp.concatenate(mixed, 1).astype(BF16)
        return carry

    for at in range(tokens // chunk):
        step(at, 0)


def body(
    light_query,
    light_keys,
    light_values,
    decay_rate,
    norm_gain,
    soft_query,
    soft_keys,
    soft_values,
    segment_ids,
):
    places = lax.axis_size("head")
    n_all = lax.axis_size("ctx") * places
    members = LOOK * places
    core = lax.rem(lax.axis_index("ctx"), LOOK)
    place = lax.axis_index("head")
    at = jnp.stack([core, place, core * places + place]).astype(jnp.int32)
    tokens, heads, width = light_query.shape
    kv_heads = soft_keys.shape[1]
    per, half, kv_half = heads // members, heads // LOOK, kv_heads // LOOK
    sid_row = segment_ids.reshape(1, tokens)

    def partner(value, k):
        pairs = [(i, i - i % members + ((i % members) ^ k)) for i in range(n_all)]
        return lax.ppermute(value, AXES, pairs)

    def across(value):
        return partner(value, places)

    def onward(value):
        return lax.ppermute(value, AXES, [(i, i + members) for i in range(n_all - members)])

    def shape(*dims):
        return jax.ShapeDtypeStruct(dims, BF16)

    def room(*dims, dtype=BF16):
        return pltpu.VMEM(dims, dtype)

    def semaphores(count):
        return pltpu.SemaphoreType.DMA((count,))

    pay = shape(2 * kv_half * tokens + TAIL, width)
    state = shape(per * width + TAIL, width)
    by_head = shape(heads, tokens, width)
    half_out = shape(tokens, half, width)
    slots = room(members, *state.shape)

    keep, give, query_give = call(
        pack_kernel, "pack", 2, 8, [SMEM, VMEM, ANY, ANY, ANY], [pay, pay, half_out], [VMEM, VMEM, ANY],
        [room(tokens, kv_heads, width)] * 2 + [room(kv_heads, tokens, width), semaphores(3)],
    )(at, sid_row, soft_keys, soft_values, soft_query)
    theirs = across(give)
    made = call(
        functools.partial(source_kernel, members), "source", 5, 16, [SMEM, SMEM, VMEM, ANY, ANY],
        [state] * members + [by_head] * 2, [VMEM] * (members + 2),
        [room(tokens, heads, width)] * 2 + [semaphores(2)],
    )(at, decay_rate, sid_row, light_keys, light_values)
    states, keys_by_head, values_by_head = made[:members], made[members], made[members + 1]
    states = [states[0]] + [partner(states[k], k) for k in range(1, members)]
    keep_before, theirs_before = onward(keep), onward(theirs)
    query_got = across(query_give)

    left = call(
        prep_kernel, "prep", 4, 16, [SMEM, VMEM, VMEM, VMEM], shape(heads, tokens, tokens + width), VMEM
    )(decay_rate, sid_row, light_query, keys_by_head)

    mixed = call(
        functools.partial(mix_kernel, places), "mix", 1, 8, [SMEM] + [VMEM] * 4,
        [shape(4, *pay.shape)] + [shape(3, *pay.shape)] * (places - 1), [VMEM] * places,
    )(at, keep, theirs, keep_before, theirs_before)
    home, parcels = mixed[0], mixed[1:]
    parcels = [partner(parcels[k - 1], k) for k in range(1, places)]

    ending = call(
        functools.partial(ending_kernel, members, tokens), "ending", 1, 8, [SMEM] * 2 + [VMEM] * members, state, VMEM, [slots]
    )(at, decay_rate, *states)
    entry = onward(ending)
    entries = call(
        functools.partial(prefix_kernel, members, tokens), "prefix", 1, 12, [SMEM] * 2 + [VMEM] * (members + 1),
        [state] * members, [VMEM] * members, [slots, slots],
    )(at, decay_rate, entry, *states)
    entries = [entries[0]] + [partner(entries[k], k) for k in range(1, members)]

    share = half // kv_half
    blocks = 2 * places + 1
    limit = (blocks * tokens * tokens * share * 14 + 8 * half_out.size) / 2**20 + 8

    def soft(own, query):
        return call(
            functools.partial(soft_kernel, places, tokens, own), "soft", 5, limit, [SMEM] + [VMEM] * (places + 1), half_out, VMEM,
            [room(tokens * share, tokens), room(blocks * tokens, width), room(tokens * share, tokens, dtype=F32)],
        )(at, query, home, *parcels)

    soft_got = across(soft(False, query_got))
    soft_kept = soft(True, soft_query)

    whole = shape(tokens, heads, width)
    return tuple(
        call(
            functools.partial(final_kernel, members), "final", 4, 16, [SMEM] * 2 + [VMEM] * (6 + members), [whole, whole],
            [VMEM, VMEM], [room(heads, tokens, width)],
        )(at, decay_rate, sid_row, norm_gain, left, values_by_head, soft_kept, soft_got, *entries)
    )


def solution(mesh):
    placed = P(("ctx", "head"), None, None)
    return jax.shard_map(
        body,
        mesh=mesh,
        in_specs=(placed, placed, placed, P(), P(), placed, placed, placed, P(("ctx", "head"))),
        out_specs=(placed, placed),
        check_vma=False,
    )
```

```python
import functools
import math

import jax
import jax.numpy as jnp
from jax import lax
from jax.experimental import pallas as pl
from jax.experimental.pallas import tpu as pltpu
from jax.sharding import PartitionSpec as P

LOOK = 2
NEG_FILL = -1e30
NORM_EPS = 1e-06
TAIL = 16
F32 = jnp.float32
BF16 = jnp.bfloat16
AXES = ("ctx", "head")
VMEM = pl.BlockSpec(memory_space=pltpu.VMEM)
SMEM = pl.BlockSpec(memory_space=pltpu.SMEM)
ANY = pl.BlockSpec(memory_space=pl.ANY)
HBM = pl.BlockSpec(memory_space=pltpu.HBM)


def call(kernel, name, micros, limit_mib, ins, outs, out_specs, scratch=(), aliases=None, after=()):
    count = len(ins)

    def run(*refs):
        kernel(*refs[:count], *refs[count + len(after) :])

    made = pl.pallas_call(
        run,
        out_shape=outs,
        in_specs=list(ins) + [ANY] * len(after),
        out_specs=out_specs,
        scratch_shapes=list(scratch),
        input_output_aliases=aliases or {},
        compiler_params=pltpu.CompilerParams(vmem_limit_bytes=int(limit_mib * 1024 * 1024)),
        cost_estimate=pl.CostEstimate(flops=int(micros * 1e9), bytes_accessed=0, transcendentals=0),
        name=name,
    )
    return lambda *args: made(*args, *after)


def column(row):
    size = row.shape[1]
    return jnp.transpose(jnp.broadcast_to(row, (size, size)))


def dot(left, right, contract):
    return lax.dot_general(left, right, (contract, ((), ())), preferred_element_type=F32)


def split(value):
    high = value.astype(BF16)
    return high, (value - high.astype(F32)).astype(BF16)


def source_kernel(places, at_ref, rate_hbm, sid_hbm, key_hbm, value_hbm, soft_key_hbm, soft_value_hbm, soft_query_hbm, *rest):
    outs, rest = rest[:places], rest[places:]
    keys_by_head, values_by_head, mine_ref, other_ref, give_ref, rate_ref, sid_ref, key_in, value_in, soft_key_in, soft_value_in, stage, sems = rest
    heads, tokens, width = keys_by_head.shape
    per, half = heads // places, heads // LOOK
    kv_heads = soft_key_in.shape[1]
    kv_half = kv_heads // LOOK
    rows = mine_ref.shape[0]
    core, place = at_ref[0], at_ref[1]
    theirs = pl.ds(pl.multiple_of((LOOK - 1 - core) * half, half), half)
    moves = (
        (soft_key_hbm, soft_key_in),
        (soft_value_hbm, soft_value_in),
        (sid_hbm, sid_ref),
        (rate_hbm, rate_ref),
        (key_hbm, key_in),
        (value_hbm, value_in),
        (soft_query_hbm.at[:, theirs, :], give_ref.at[pl.ds(rows // half, tokens)]),
    )
    copies = [pltpu.make_async_copy(src, dst, sems.at[n]) for n, (src, dst) in enumerate(moves)]
    for copy in copies:
        copy.start()
    for at, ref in enumerate((soft_key_in, soft_value_in)):
        copies[at].wait()
        stage[...] = jnp.swapaxes(ref[...], 0, 1)
        for j in range(kv_half):
            start = (at * kv_half + j) * tokens
            mine_ref[pl.ds(start, tokens), :] = stage[core * kv_half + j]
            block = stage[(LOOK - 1 - core) * kv_half + j]
            other_ref[pl.ds(start, tokens), :] = block
            give_ref[pl.ds(start // half, tokens // half)] = block.reshape(tokens // half, half, width)
    copies[2].wait()
    sid_row = (sid_ref[...] + 1).astype(F32)
    tail = jnp.broadcast_to(sid_row, (TAIL, tokens)).astype(BF16)
    for ref in (mine_ref, other_ref):
        ref[pl.ds(2 * kv_half * tokens, TAIL), :] = tail
    give_ref[pl.ds(2 * kv_half * tokens // half, TAIL // half)] = tail.reshape(TAIL // half, half, tokens)
    open_row = (sid_row == jnp.max(sid_row, axis=1, keepdims=True)).astype(F32)
    behind = (tokens - 1 - lax.broadcasted_iota(jnp.int32, (1, tokens), 1)).astype(F32)
    copies[3].wait()
    copies[4].wait()
    keys_by_head[...] = jnp.swapaxes(key_in[...], 0, 1)
    copies[5].wait()
    values_by_head[...] = jnp.swapaxes(value_in[...], 0, 1)
    for k in range(places):
        for j in range(per):
            head = (place ^ k) * per + j
            values = values_by_head[head]
            weighted = jnp.transpose(keys_by_head[head].astype(F32)) * (open_row * jnp.exp(-rate_ref[head] * behind))
            high, low = split(weighted)
            state = dot(jnp.concatenate([high, low], 1), jnp.concatenate([values, values], 0), ((1,), (0,)))
            outs[k][pl.ds(j * width, width), :] = state.astype(BF16)
        outs[k][pl.ds(per * width, TAIL), :] = tail
    copies[6].wait()


def mix_kernel(places, at_ref, mine_ref, got_ref, before_ref, theirs_before_ref, home_ref, *outs):
    core, place = at_ref[0], at_ref[1]
    rows, width = mine_ref.shape
    heads = got_ref.shape[1]
    home_ref[2 * core] = mine_ref[...]
    home_ref[2 * core + 1] = before_ref[...]
    home_ref[2 * (1 - core)] = got_ref[pl.ds(0, rows // heads)].reshape(rows, width)
    home_ref[2 * (1 - core) + 1] = theirs_before_ref[...]
    for k in range(1, places):
        out = outs[k - 1]
        later = ((place ^ k) > place).astype(jnp.int32)
        out[0] = home_ref[0]
        out[1] = home_ref[3]
        out[2] = home_ref[1 + later]


def gather_slots(places, at_ref, pays, slots):
    for k in range(places):
        slots[at_ref[1] ^ k] = pays[k][...]


def last_of(pay, per, width):
    return jnp.max(pay[pl.ds(per * width, TAIL), :].astype(F32), axis=(0, 1), keepdims=True)


def advance(pay, per, width, span, rates, state, last):
    now = last_of(pay, per, width)
    same = (now == last).astype(F32)
    state = [
        pay[pl.ds(j * width, width), :].astype(F32) + (same * jnp.exp(jnp.full((1, width), -rates[j] * span, F32))) * state[j]
        for j in range(per)
    ]
    return state, now


def store_state(ref, state, last):
    width = ref.shape[1]
    for j, value in enumerate(state):
        ref[pl.ds(j * width, width), :] = value.astype(BF16)
    ref[pl.ds(len(state) * width, TAIL), :] = jnp.broadcast_to(last, (TAIL, width)).astype(BF16)


def ending_kernel(places, tokens, at_ref, rate_ref, *rest):
    pays, out_ref, slots = rest[:places], rest[places], rest[places + 1]
    width = out_ref.shape[1]
    per = (out_ref.shape[0] - TAIL) // width
    gather_slots(places, at_ref, pays, slots)
    rates = [rate_ref[at_ref[1] * per + j] for j in range(per)]
    state = [jnp.zeros((width, width), F32)] * per
    last = jnp.zeros((1, 1), F32)
    for block in range(places):
        state, last = advance(slots.at[block], per, width, tokens, rates, state, last)
    store_state(out_ref, state, last)


def prefix_kernel(places, tokens, at_ref, rate_ref, *rest):
    ahead, pays, outs = rest[:LOOK], rest[LOOK : LOOK + places], rest[LOOK + places : LOOK + 2 * places]
    slots, results = rest[LOOK + 2 * places :]
    width = ahead[0].shape[1]
    per = (ahead[0].shape[0] - TAIL) // width
    gather_slots(places, at_ref, pays, slots)
    rates = [rate_ref[at_ref[1] * per + j] for j in range(per)]
    state = [ahead[-1][pl.ds(j * width, width), :].astype(F32) for j in range(per)]
    last = last_of(ahead[-1], per, width)
    for group in reversed(ahead[:-1]):
        state, last = advance(group, per, width, places * tokens, rates, state, last)
    for block in range(places):
        store_state(results.at[block], state, last)
        if block < places - 1:
            state, last = advance(slots.at[block], per, width, tokens, rates, state, last)
    for k in range(places):
        outs[k][...] = results[at_ref[1] ^ k]


def prep_kernel(rate_ref, sid_ref, query_ref, keys_by_head, left_ref):
    heads, tokens, _ = keys_by_head.shape
    sid_row = (sid_ref[...] + 1).astype(F32)
    row_at = lax.broadcasted_iota(jnp.int32, (tokens, tokens), 0)
    lane = lax.broadcasted_iota(jnp.int32, (tokens, tokens), 1)
    allowed = ((row_at >= lane) & (column(sid_row) == sid_row)).astype(F32)
    ahead = (lax.broadcasted_iota(jnp.int32, (1, tokens), 1) + 1).astype(F32)
    left_ref[:, :, tokens:] = jnp.swapaxes(query_ref[...], 0, 1)
    for head in range(heads):
        weights = dot(left_ref[head, :, tokens:], keys_by_head[head], ((1,), (1,)))
        weights = weights * allowed * jnp.exp(rate_ref[head] * ahead)
        left_ref[head, :, :tokens] = weights.astype(BF16)


def final_kernel(places, at_ref, rate_ref, sid_ref, gain_ref, left_ref, values_by_head, keep_ref, *rest):
    pays, rest = rest[:places], rest[places:]
    light_hbm, soft_hbm, by_head, stage, sems = rest
    heads, tokens, width = values_by_head.shape
    half, per = heads // LOOK, heads // places
    core, place = at_ref[0], at_ref[1]

    def columns(which):
        return pl.ds(pl.multiple_of(which * half, half), half)

    copies = [pltpu.make_async_copy(keep_ref, soft_hbm.at[:, columns(core), :], sems.at[LOOK])]
    copies[0].start()
    sid_column = column((sid_ref[...] + 1).astype(F32))
    entry = last_of(pays[0], per, width)
    continues = (sid_column == entry).astype(BF16)
    ahead = (lax.broadcasted_iota(jnp.int32, (tokens, 1), 0) + 1).astype(F32)
    span = places // LOOK
    for part in range(LOOK):
        which = (place // span) ^ part
        for k in range(part * span, (part + 1) * span):
            for j in range(per):
                head = (place ^ k) * per + j
                left = jnp.concatenate([left_ref[head, :, :tokens], left_ref[head, :, tokens:] * continues], 1)
                right = jnp.concatenate([values_by_head[head], pays[k][pl.ds(j * width, width), :]], 0)
                raw = dot(left, right, ((1,), (0,)))
                lead = jnp.exp(-rate_ref[head] * ahead)
                mean_square = jnp.mean(raw * raw, axis=1, keepdims=True) * (lead * lead)
                out = raw * (lead * lax.rsqrt(mean_square + NORM_EPS)) * gain_ref[pl.ds(head, 1), :]
                by_head[head] = out.astype(BF16)
        stage[part] = jnp.swapaxes(by_head[pl.ds(which * half, half)], 0, 1)
        copies.append(pltpu.make_async_copy(stage.at[part], light_hbm.at[:, columns(which), :], sems.at[part]))
        copies[-1].start()
    for copy in copies:
        copy.wait()


def beside_kernel(at_ref, got_ref, _, out_hbm, sem):
    half = got_ref.shape[1]
    columns = pl.ds(pl.multiple_of((LOOK - 1 - at_ref[0]) * half, half), half)
    copy = pltpu.make_async_copy(got_ref, out_hbm.at[:, columns, :], sem)
    copy.start()
    copy.wait()


class Soft:
    def __init__(self, places, at_ref, tokens, share, heads, rows, marks, codes, fills):
        self.places, self.core, self.place = places, at_ref[0], at_ref[1]
        self.tokens, self.share, self.heads, self.rows = tokens, share, heads, rows
        self.kv_heads = heads // share
        self.marks, self.codes, self.fills = marks, codes, fills
        self.lane = lax.broadcasted_iota(jnp.int32, (tokens, tokens), 1)

    def spread(self, value):
        tokens, share = self.tokens, self.share
        value = jnp.broadcast_to(value.reshape(tokens, 1, tokens), (tokens, share, tokens))
        return value.reshape(tokens * share, tokens)

    def sids(self, pick):
        ref, slot = pick
        return column(ref[slot, pl.ds(2 * self.kv_heads * self.tokens, TAIL), :].astype(F32)[0:1, :])

    def far(self, block, ks, pays):
        picks = []
        for k, pay in zip(ks, pays):
            later = ((self.place ^ k) > self.place).astype(jnp.int32)
            picks.append((pay, 2 * later * (1 - block)))
            picks.append((pay, 1 + (1 - later) * block))
        return picks

    def setup(self, picks, own, causal):
        tokens, lanes = self.tokens, self.lane.astype(F32)
        for at, pick in enumerate(picks):
            self.codes[pl.ds(at * tokens, tokens), :] = (self.sids(pick) == lanes).astype(BF16)
        self.marks[...] = self.spread(jnp.where(self.sids(own) == lanes, 0.0, NEG_FILL)).astype(BF16)
        if causal:
            row_at = lax.broadcasted_iota(jnp.int32, (tokens, tokens), 0)
            self.fills[...] = self.spread(jnp.where(row_at >= self.lane, 0.0, NEG_FILL))

    def query(self, ref, first_token, first_head):
        wide = ref[pl.ds(first_token, self.tokens), pl.ds(first_head, self.heads), :].astype(F32)
        width, share = wide.shape[2], self.share
        return [
            wide[:, g * share : (g + 1) * share, :].reshape(self.tokens * share, width).astype(BF16)
            for g in range(self.kv_heads)
        ]

    def scores(self, g, query, picks, causal):
        tokens = self.tokens
        query = jnp.concatenate([query, self.marks[...]], 1)
        keys = jnp.concatenate([ref[slot, pl.ds(g * tokens, tokens), :] for ref, slot in picks], 0)
        codes = self.codes[pl.ds(0, len(picks) * tokens), :]
        scores = dot(query, jnp.concatenate([keys, codes], 1), ((1,), (1,)))
        if causal:
            last = (len(picks) - 1) * tokens
            scores = jnp.concatenate([scores[:, :last], scores[:, last:] + self.fills[...]], 1)
        return scores

    def mixed(self, g, probs, picks):
        tokens = self.tokens
        rows = pl.ds((self.kv_heads + g) * tokens, tokens)
        values = jnp.concatenate([ref[slot, rows, :] for ref, slot in picks], 0)
        return dot(probs.astype(BF16), jnp.concatenate([values, jnp.ones_like(values)], 1), ((1,), (0,)))


    def queries(self, own, got_ref, query_ref):
        if own:
            return self.query(query_ref, 0, pl.multiple_of(self.core * self.heads, self.heads))
        return self.query(got_ref, self.rows // self.heads, 0)

    def added(self, g, query, picks, sums, before):
        width = before.shape[1]
        factor = width ** (-0.5) * math.log2(math.e)
        scores = self.scores(g, query, picks, False)
        peak = jnp.maximum(before, jnp.max(scores, axis=1, keepdims=True))
        probs = jnp.exp2((scores - peak[:, 0:1]) * factor)
        scale = jnp.exp2((before - peak) * factor)
        return self.mixed(g, probs, picks) + sums * jnp.concatenate([scale, scale], 1), peak


def home_kernel(places, share, at_ref, got_ref, query_ref, home_ref, sums_ref, peaks_ref, *rooms):
    tokens, width = query_ref.shape[0], query_ref.shape[2]
    soft = Soft(places, at_ref, tokens, share, got_ref.shape[1], home_ref.shape[1], *rooms)
    factor = width ** (-0.5) * math.log2(math.e)
    for own in (False, True):
        block = soft.core if own else 1 - soft.core
        mine = (home_ref, 2 * block)
        picks = [(home_ref, 1 - block), (home_ref, 3), mine]
        soft.setup(picks, mine, True)
        for g, query in enumerate(soft.queries(own, got_ref, query_ref)):
            scores = soft.scores(g, query, picks, True)
            peak = jnp.max(scores, axis=1, keepdims=True)
            at = (soft.kv_heads if own else 0) + g
            sums_ref[at] = soft.mixed(g, jnp.exp2((scores - peak) * factor), picks)
            peaks_ref[at] = jnp.broadcast_to(peak, (tokens * share, width))


def near_kernel(places, near, share, at_ref, got_ref, query_ref, home_ref, sums_in, peaks_in, *rest):
    pays, sums_ref, peaks_ref = rest[: len(near)], rest[len(near)], rest[len(near) + 1]
    soft = Soft(places, at_ref, query_ref.shape[0], share, got_ref.shape[1], home_ref.shape[1], *rest[len(near) + 2 :])
    for own in (False, True):
        block = soft.core if own else 1 - soft.core
        picks = soft.far(block, near, pays)
        soft.setup(picks, (home_ref, 2 * block), False)
        for g, query in enumerate(soft.queries(own, got_ref, query_ref)):
            at = (soft.kv_heads if own else 0) + g
            sums_ref[at], peaks_ref[at] = soft.added(g, query, picks, sums_in[at], peaks_in[at])


def far_kernel(places, far, share, at_ref, got_ref, query_ref, home_ref, sums_ref, peaks_ref, *rest):
    pays, outs, rooms = rest[: len(far)], rest[len(far) : len(far) + 2], rest[len(far) + 2 :]
    tokens, heads, width = query_ref.shape[0], got_ref.shape[1], query_ref.shape[2]
    soft = Soft(places, at_ref, tokens, share, heads, home_ref.shape[1], *rooms)
    for own in (False, True):
        block = soft.core if own else 1 - soft.core
        picks = soft.far(block, far, pays)
        soft.setup(picks, (home_ref, 2 * block), False)
        mixed = []
        for g, query in enumerate(soft.queries(own, got_ref, query_ref)):
            at = (soft.kv_heads if own else 0) + g
            out, _ = soft.added(g, query, picks, sums_ref[at], peaks_ref[at])
            mixed.append((out[:, :width] / out[:, width:]).reshape(tokens, share, width))
        outs[own][...] = jnp.concatenate(mixed, 1).astype(BF16)


def body(
    light_query,
    light_keys,
    light_values,
    decay_rate,
    norm_gain,
    soft_query,
    soft_keys,
    soft_values,
    segment_ids,
):
    places = lax.axis_size("head")
    n_all = lax.axis_size("ctx") * places
    members = LOOK * places
    core = lax.rem(lax.axis_index("ctx"), LOOK)
    place = lax.axis_index("head")
    at = jnp.stack([core, place, core * places + place]).astype(jnp.int32)
    tokens, heads, width = light_query.shape
    kv_heads = soft_keys.shape[1]
    per, half, kv_half = heads // places, heads // LOOK, kv_heads // LOOK
    sid_row = segment_ids.reshape(1, tokens)

    def partner(value, k):
        pairs = [(i, i - i % members + ((i % members) ^ k)) for i in range(n_all)]
        return lax.ppermute(value, AXES, pairs)

    def across(value):
        return partner(value, places)

    def to_places(values):
        return [values[0]] + [partner(values[k], k) for k in range(1, places)]

    def onward(value, groups):
        step = groups * places
        return lax.ppermute(value, AXES, [(i, i + step) for i in range(n_all - step)])

    def onward_across(value):
        pairs = [(i, i + members + (places if i // places % LOOK == 0 else -places)) for i in range(n_all - members)]
        return lax.ppermute(value, AXES, pairs)

    def shape(*dims):
        return jax.ShapeDtypeStruct(dims, BF16)

    def room(*dims, dtype=BF16):
        return pltpu.VMEM(dims, dtype)

    def semaphores(count):
        return pltpu.SemaphoreType.DMA((count,))

    pay = shape(2 * kv_half * tokens + TAIL, width)
    given = shape(pay.shape[0] // half + tokens, half, width)
    state = shape(per * width + TAIL, width)
    by_head = shape(heads, tokens, width)
    half_out = shape(tokens, half, width)
    slots = room(places, *state.shape)
    sid_room = room(1, tokens, dtype=jnp.int32)

    def held(value):
        return pltpu.with_memory_space_constraint(value, pltpu.HBM)

    made = call(
        functools.partial(source_kernel, places), "source", 0, 16, [SMEM] + [HBM] * 7,
        [state] * places + [by_head] * 2 + [pay, pay, given], [VMEM] * (places + 5),
        [pltpu.SMEM((heads,), F32), sid_room] + [room(tokens, heads, width)] * 2 + [room(tokens, kv_heads, width)] * 2
        + [room(kv_heads, tokens, width), semaphores(7)],
    )(at, *[held(x) for x in (decay_rate, sid_row, light_keys, light_values, soft_keys, soft_values, soft_query)])
    keys_by_head, values_by_head, mine, other, give = made[places:]
    states = to_places(made[:places])
    got = across(give)
    before = onward(mine, LOOK)
    theirs_before = onward_across(other)

    left = call(
        prep_kernel, "prep", 0, 16, [SMEM, VMEM, VMEM, VMEM], shape(heads, tokens, tokens + width), VMEM
    )(decay_rate, sid_row, light_query, keys_by_head)
    mixed = call(
        functools.partial(mix_kernel, places), "mix", 0, 8, [SMEM] + [VMEM] * 4,
        [shape(4, *pay.shape)] + [shape(3, *pay.shape)] * (places - 1), [VMEM] * places, after=[left, *states[places // 2 + 1 :]],
    )(at, mine, got, before, theirs_before)
    home = mixed[0]
    parcels = to_places(mixed)

    ending = call(
        functools.partial(ending_kernel, places, tokens), "ending", 0, 8, [SMEM] * 2 + [VMEM] * places, state, VMEM,
        [slots], after=[home],
    )(at, decay_rate, *states)
    ahead = [onward(ending, groups) for groups in range(1, LOOK + 1)]
    share = half // kv_half
    near, far = range(1, places // 2 + 1), range(places // 2 + 1, places)
    queries = tokens * share

    def soft_rooms(blocks):
        return [room(queries, tokens), room(blocks * tokens, width), room(queries, tokens, dtype=F32)]

    def limit(blocks):
        return (blocks * tokens * queries * 14 + 8 * half_out.size) / 2**20 + 8

    sums_like = [
        jax.ShapeDtypeStruct((LOOK * kv_half, queries, 2 * width), F32),
        jax.ShapeDtypeStruct((LOOK * kv_half, queries, width), F32),
    ]
    sums, peaks = call(
        functools.partial(home_kernel, places, share), "home", 0, limit(3), [SMEM] + [VMEM] * 3, sums_like, [VMEM, VMEM],
        soft_rooms(3), after=[ending],
    )(at, got, soft_query, home)
    prefixed = call(
        functools.partial(prefix_kernel, places, tokens), "prefix", 0, 12, [SMEM] * 2 + [VMEM] * (places + LOOK),
        [state] * places, [VMEM] * places, [slots, slots], after=[sums],
    )(at, decay_rate, *ahead, *states)
    entries = to_places(prefixed)

    sums, peaks = call(
        functools.partial(near_kernel, places, near, share), "near", 30, limit(2 * len(near)), [SMEM] + [VMEM] * (5 + len(near)),
        sums_like, [VMEM, VMEM], soft_rooms(2 * len(near)), aliases={4: 0, 5: 1}, after=[prefixed[0]],
    )(at, got, soft_query, home, sums, peaks, *[parcels[k] for k in near])

    soft_theirs, soft_kept = call(
        functools.partial(far_kernel, places, far, share), "far", 0, limit(2 * len(far)), [SMEM] + [VMEM] * (5 + len(far)),
        [half_out] * 2, [VMEM] * 2, soft_rooms(2 * len(far)),
    )(at, got, soft_query, home, sums, peaks, *[parcels[k] for k in far])
    soft_got = across(soft_theirs)

    whole = shape(tokens, heads, width)
    light_out, soft_out = call(
        functools.partial(final_kernel, places), "final", 15, 16, [SMEM] * 2 + [VMEM] * (5 + places), [whole, whole],
        [HBM, HBM], [room(heads, tokens, width), room(LOOK, tokens, half, width), semaphores(LOOK + 1)],
    )(at, decay_rate, sid_row, norm_gain, left, values_by_head, soft_kept, *entries)
    soft_out = call(
        beside_kernel, "beside", 0, 8, [SMEM, VMEM, HBM], whole, HBM, [pltpu.SemaphoreType.DMA], aliases={2: 0}
    )(at, soft_got, soft_out)
    return (light_out, soft_out)


def solution(mesh):
    placed = P(("ctx", "head"), None, None)
    return jax.shard_map(
        body,
        mesh=mesh,
        in_specs=(placed, placed, placed, P(), P(), placed, placed, placed, P(("ctx", "head"))),
        out_specs=(placed, placed),
        check_vma=False,
    )
```

```python
import functools
import math

import jax
import jax.numpy as jnp
from jax import lax
from jax.experimental import pallas as pl
from jax.experimental.pallas import tpu as pltpu
from jax.sharding import PartitionSpec as P

LOOK = 2
NEG_FILL = -1e30
NORM_EPS = 1e-06
TAIL = 16
F32 = jnp.float32
BF16 = jnp.bfloat16
AXES = ("ctx", "head")
VMEM = pl.BlockSpec(memory_space=pltpu.VMEM)
SMEM = pl.BlockSpec(memory_space=pltpu.SMEM)
ANY = pl.BlockSpec(memory_space=pl.ANY)
HBM = pl.BlockSpec(memory_space=pltpu.HBM)


def call(kernel, name, micros, limit_mib, ins, outs, out_specs, scratch=(), aliases=None, after=()):
    count = len(ins)

    def run(*refs):
        kernel(*refs[:count], *refs[count + len(after) :])

    made = pl.pallas_call(
        run,
        out_shape=outs,
        in_specs=list(ins) + [ANY] * len(after),
        out_specs=out_specs,
        scratch_shapes=list(scratch),
        input_output_aliases=aliases or {},
        compiler_params=pltpu.CompilerParams(vmem_limit_bytes=int(limit_mib * 1024 * 1024)),
        cost_estimate=pl.CostEstimate(flops=int(micros * 1e9), bytes_accessed=0, transcendentals=0),
        name=name,
    )
    return lambda *args: made(*args, *after)


def column(row):
    size = row.shape[1]
    return jnp.transpose(jnp.broadcast_to(row, (size, size)))


def dot(left, right, contract):
    return lax.dot_general(left, right, (contract, ((), ())), preferred_element_type=F32)


def odd(place):
    for shift in (8, 4, 2, 1):
        place = place ^ (place >> shift)
    return place & 1


def share_of(places, place):
    return odd(place) * (places // 2) + (place >> 1)


def split(value):
    high = value.astype(BF16)
    return high, (value - high.astype(F32)).astype(BF16)


def source_kernel(places, at_ref, rate_hbm, sid_hbm, key_hbm, value_hbm, soft_key_hbm, soft_value_hbm, soft_query_hbm, *rest):
    outs, rest = rest[:places], rest[places:]
    keys_by_head, values_by_head, pair_ref, give_ref, rate_ref, sid_ref, key_in, value_in, soft_key_in, soft_value_in, stage, sems = rest
    heads, tokens, width = keys_by_head.shape
    per, half = heads // places, heads // LOOK
    kv_heads = soft_key_in.shape[1]
    kv_half = kv_heads // LOOK
    span = 2 * kv_half * tokens
    rows = span + TAIL
    core, place = at_ref[0], at_ref[1]
    mine = pl.multiple_of(core * span, TAIL)
    theirs = pl.ds(pl.multiple_of((LOOK - 1 - core) * half, half), half)
    moves = (
        (soft_key_hbm, soft_key_in),
        (soft_value_hbm, soft_value_in),
        (sid_hbm, sid_ref),
        (rate_hbm, rate_ref),
        (key_hbm, key_in),
        (value_hbm, value_in),
        (soft_query_hbm.at[:, theirs, :], give_ref.at[pl.ds(rows // half, tokens)]),
    )
    copies = [pltpu.make_async_copy(src, dst, sems.at[n]) for n, (src, dst) in enumerate(moves)]
    for copy in copies:
        copy.start()
    for at, ref in enumerate((soft_key_in, soft_value_in)):
        copies[at].wait()
        stage[...] = jnp.swapaxes(ref[...], 0, 1)
        for j in range(kv_half):
            start = (at * kv_half + j) * tokens
            pair_ref[pl.ds(mine + start, tokens), :] = stage[core * kv_half + j]
            block = stage[(LOOK - 1 - core) * kv_half + j]
            give_ref[pl.ds(start // half, tokens // half)] = block.reshape(tokens // half, half, width)
    copies[2].wait()
    sid_row = (sid_ref[...] + 1).astype(F32)
    tail = jnp.broadcast_to(sid_row, (TAIL, tokens)).astype(BF16)
    pair_ref[pl.ds(LOOK * span, TAIL), :] = tail
    give_ref[pl.ds(2 * kv_half * tokens // half, TAIL // half)] = tail.reshape(TAIL // half, half, tokens)
    open_row = (sid_row == jnp.max(sid_row, axis=1, keepdims=True)).astype(F32)
    behind = (tokens - 1 - lax.broadcasted_iota(jnp.int32, (1, tokens), 1)).astype(F32)
    copies[3].wait()
    copies[4].wait()
    keys_by_head[...] = jnp.swapaxes(key_in[...], 0, 1)
    copies[5].wait()
    values_by_head[...] = jnp.swapaxes(value_in[...], 0, 1)
    for k in range(places):
        for j in range(per):
            head = share_of(places, place ^ k) * per + j
            values = values_by_head[head]
            weighted = jnp.transpose(keys_by_head[head].astype(F32)) * (open_row * jnp.exp(-rate_ref[head] * behind))
            high, low = split(weighted)
            state = dot(jnp.concatenate([high, low], 1), jnp.concatenate([values, values], 0), ((1,), (0,)))
            outs[k][pl.ds(j * width, width), :] = state.astype(BF16)
        outs[k][pl.ds(per * width, TAIL), :] = tail
        outs[k][pl.ds(per * width + TAIL, TAIL), :] = tail
    copies[6].wait()


def pair_kernel(at_ref, got_ref, _, pair_ref):
    heads = got_ref.shape[1]
    width = pair_ref.shape[1]
    span = (pair_ref.shape[0] - TAIL) // LOOK
    other = 1 - at_ref[0]
    pair_ref[pl.ds(pl.multiple_of(other * span, TAIL), span), :] = got_ref[pl.ds(0, span // heads)].reshape(span, width)
    theirs = got_ref[pl.ds(span // heads, TAIL // heads)].reshape(TAIL, width)
    row_at = lax.broadcasted_iota(jnp.int32, (TAIL, width), 0)
    mine = pair_ref[pl.ds(LOOK * span, TAIL), :].astype(F32)
    tail = jnp.where(row_at // (TAIL // LOOK) == other, theirs.astype(F32), mine)
    pair_ref[pl.ds(LOOK * span, TAIL), :] = tail.astype(BF16)


def mix_kernel(places, at_ref, pair_ref, before_ref, *rest):
    home_ref, outs = rest[-places], rest[1 - places :]
    width = pair_ref.shape[1]
    span = (pair_ref.shape[0] - TAIL) // LOOK
    place = at_ref[1]
    for back, ref in enumerate((pair_ref, before_ref)):
        tails = ref[pl.ds(LOOK * span, TAIL), :].astype(F32)
        for block in range(LOOK):
            slot = LOOK * block + back
            home_ref[slot, pl.ds(0, span), :] = ref[pl.ds(block * span, span), :]
            row = block * (TAIL // LOOK)
            home_ref[slot, pl.ds(span, TAIL), :] = jnp.broadcast_to(tails[row : row + 1], (TAIL, width)).astype(BF16)
    for k in range(1, places):
        out = outs[k - 1]
        later = ((place ^ k) > place).astype(jnp.int32)
        out[0] = home_ref[0]
        out[1] = home_ref[3]
        out[2] = home_ref[1 + later]


def gather_slots(places, at_ref, pays, slots):
    for k in range(places):
        slots[at_ref[1] ^ k] = pays[k][pl.ds(0, slots.shape[1]), :]


def last_of(pay, per, width):
    return jnp.max(pay[pl.ds(per * width, TAIL), :].astype(F32), axis=(0, 1), keepdims=True)


def advance(pay, per, width, span, rates, state, last):
    now = last_of(pay, per, width)
    same = (now == last).astype(F32)
    state = [
        pay[pl.ds(j * width, width), :].astype(F32) + (same * jnp.exp(jnp.full((1, width), -rates[j] * span, F32))) * state[j]
        for j in range(per)
    ]
    return state, now


def store_state(ref, state, last):
    width = ref.shape[1]
    for j, value in enumerate(state):
        ref[pl.ds(j * width, width), :] = value.astype(BF16)
    ref[pl.ds(len(state) * width, TAIL), :] = jnp.broadcast_to(last, (TAIL, width)).astype(BF16)


def ending_kernel(places, tokens, at_ref, rate_ref, *rest):
    pays, out_ref, slots = rest[:places], rest[places], rest[places + 1]
    width = out_ref.shape[1]
    per = (out_ref.shape[0] - TAIL) // width
    gather_slots(places, at_ref, pays, slots)
    rates = [rate_ref[share_of(places, at_ref[1]) * per + j] for j in range(per)]
    state = [jnp.zeros((width, width), F32)] * per
    last = jnp.zeros((1, 1), F32)
    for block in range(places):
        state, last = advance(slots.at[block], per, width, tokens, rates, state, last)
    store_state(out_ref, state, last)


def prefix_kernel(places, tokens, at_ref, rate_ref, *rest):
    ahead, pays, outs = rest[:LOOK], rest[LOOK : LOOK + places], rest[LOOK + places : LOOK + 2 * places]
    slots, results = rest[LOOK + 2 * places :]
    width = ahead[0].shape[1]
    per = (ahead[0].shape[0] - TAIL) // width
    gather_slots(places, at_ref, pays, slots)
    rates = [rate_ref[share_of(places, at_ref[1]) * per + j] for j in range(per)]
    state = [ahead[-1][pl.ds(j * width, width), :].astype(F32) for j in range(per)]
    last = last_of(ahead[-1], per, width)
    for group in reversed(ahead[:-1]):
        state, last = advance(group, per, width, places * tokens, rates, state, last)
    for block in range(places):
        store_state(results.at[block], state, last)
        if block < places - 1:
            state, last = advance(slots.at[block], per, width, tokens, rates, state, last)
    for k in range(places):
        outs[k][...] = results[at_ref[1] ^ k]


def prep_kernel(rate_ref, sid_ref, query_ref, keys_by_head, left_ref):
    heads, tokens, _ = keys_by_head.shape
    sid_row = (sid_ref[...] + 1).astype(F32)
    row_at = lax.broadcasted_iota(jnp.int32, (tokens, tokens), 0)
    lane = lax.broadcasted_iota(jnp.int32, (tokens, tokens), 1)
    allowed = ((row_at >= lane) & (column(sid_row) == sid_row)).astype(F32)
    ahead = (lax.broadcasted_iota(jnp.int32, (1, tokens), 1) + 1).astype(F32)
    left_ref[:, :, tokens:] = jnp.swapaxes(query_ref[...], 0, 1)
    for head in range(heads):
        weights = dot(left_ref[head, :, tokens:], keys_by_head[head], ((1,), (1,)))
        weights = weights * allowed * jnp.exp(rate_ref[head] * ahead)
        left_ref[head, :, :tokens] = weights.astype(BF16)


class Light:
    def __init__(self, places, at_ref, rate_ref, sid_ref, gain_ref, left_ref, values_by_head, pay):
        self.rate_ref, self.gain_ref, self.left_ref, self.values_by_head = rate_ref, gain_ref, left_ref, values_by_head
        heads, self.tokens, self.width = values_by_head.shape
        self.places, self.place, self.core = places, at_ref[1], at_ref[0]
        self.half, self.per = heads // LOOK, heads // places
        sid_column = column((sid_ref[...] + 1).astype(F32))
        self.continues = (sid_column == last_of(pay, self.per, self.width)).astype(BF16)
        self.ahead = (lax.broadcasted_iota(jnp.int32, (self.tokens, 1), 0) + 1).astype(F32)

    def columns(self, which):
        return pl.ds(pl.multiple_of(which * self.half, self.half), self.half)

    def half_out(self, ks, pays, light_hbm, by_head, stage, sem):
        which = odd(self.place ^ ks[0])
        for k, pay in zip(ks, pays):
            for j in range(self.per):
                head = share_of(self.places, self.place ^ k) * self.per + j
                tokens = self.tokens
                left = jnp.concatenate([self.left_ref[head, :, :tokens], self.left_ref[head, :, tokens:] * self.continues], 1)
                right = jnp.concatenate([self.values_by_head[head], pay[pl.ds(j * self.width, self.width), :]], 0)
                raw = dot(left, right, ((1,), (0,)))
                lead = jnp.exp(-self.rate_ref[head] * self.ahead)
                mean_square = jnp.mean(raw * raw, axis=1, keepdims=True) * (lead * lead)
                out = raw * (lead * lax.rsqrt(mean_square + NORM_EPS)) * self.gain_ref[pl.ds(head, 1), :]
                by_head[head - which * self.half] = out.astype(BF16)
        stage[...] = jnp.swapaxes(by_head[...], 0, 1)
        copy = pltpu.make_async_copy(stage, light_hbm.at[:, self.columns(which), :], sem)
        copy.start()
        return copy


def first_kernel(places, ks, at_ref, rate_ref, sid_ref, gain_ref, left_ref, values_by_head, keep_ref, _, *rest):
    pays, (light_hbm, soft_hbm, _, by_head, stage, sems) = rest[: len(ks)], rest[len(ks) :]
    light = Light(places, at_ref, rate_ref, sid_ref, gain_ref, left_ref, values_by_head, pays[0])
    copy = pltpu.make_async_copy(keep_ref, soft_hbm.at[:, light.columns(light.core), :], sems.at[0])
    copy.start()
    light.half_out(ks, pays, light_hbm, by_head, stage, sems.at[1]).wait()
    copy.wait()


def second_kernel(places, ks, at_ref, rate_ref, sid_ref, gain_ref, left_ref, values_by_head, _, *rest):
    pays, (light_hbm, done_ref, by_head, stage, sems) = rest[: len(ks)], rest[len(ks) :]
    done_ref[...] = jnp.zeros_like(done_ref)
    light = Light(places, at_ref, rate_ref, sid_ref, gain_ref, left_ref, values_by_head, pays[0])
    light.half_out(ks, pays, light_hbm, by_head, stage, sems.at[0]).wait()


def beside_kernel(at_ref, got_ref, _, out_hbm, sems):
    tokens, half, _ = got_ref.shape
    columns = pl.ds(pl.multiple_of((LOOK - 1 - at_ref[0]) * half, half), half)
    size = tokens // sems.shape[0]
    copies = []
    for n in range(sems.shape[0]):
        rows = pl.ds(n * size, size)
        copies.append(pltpu.make_async_copy(got_ref.at[rows], out_hbm.at[rows, columns, :], sems.at[n]))
        copies[-1].start()
    for copy in copies:
        copy.wait()


class Soft:
    def __init__(self, places, at_ref, query_ref, got_ref, home_ref, share, codes):
        self.core, self.place = at_ref[0], at_ref[1]
        self.tokens, _, self.width = query_ref.shape
        self.share, self.heads, self.rows = share, got_ref.shape[1], home_ref.shape[1]
        self.kv_heads = self.heads // share
        self.query_ref, self.got_ref, self.codes = query_ref, got_ref, codes
        self.lane = lax.broadcasted_iota(jnp.int32, (self.tokens, self.tokens), 1)
        self.factor = self.width ** (-0.5) * math.log2(math.e)

    def spread(self, value):
        tokens, share = self.tokens, self.share
        value = jnp.broadcast_to(value.reshape(tokens, 1, tokens), (tokens, share, tokens))
        return value.reshape(tokens * share, tokens)

    def marked(self, pick):
        ref, slot = pick
        sids = ref[slot, pl.ds(2 * self.kv_heads * self.tokens, TAIL), :].astype(F32)[0:1, :]
        return column(sids) == self.lane.astype(F32)

    def far(self, block, ks, pays):
        picks = []
        for k, pay in zip(ks, pays):
            later = ((self.place ^ k) > self.place).astype(jnp.int32)
            picks.append((pay, 2 * later * (1 - block)))
            picks.append((pay, 1 + (1 - later) * block))
        return picks

    def code(self, own, picks):
        for at, pick in enumerate(picks):
            self.codes[own, pl.ds(at * self.tokens, self.tokens), :] = self.marked(pick).astype(BF16)

    def query(self, own, g):
        tokens, share = self.tokens, self.share
        if own:
            first = pl.multiple_of(self.core * self.heads, self.heads)
            wide = self.query_ref[:, pl.ds(first, self.heads), :]
        else:
            wide = self.got_ref[pl.ds(self.rows // self.heads, tokens)]
        wide = wide.astype(F32)[:, g * share : (g + 1) * share, :]
        return wide.reshape(tokens * share, self.width).astype(BF16)

    def scores(self, own, g, marks, picks):
        tokens = self.tokens
        query = jnp.concatenate([self.query(own, g), marks], 1)
        keys = jnp.concatenate([ref[slot, pl.ds(g * tokens, tokens), :] for ref, slot in picks], 0)
        codes = self.codes[own, pl.ds(0, len(picks) * tokens), :]
        return dot(query, jnp.concatenate([keys, codes], 1), ((1,), (1,)))

    def probs(self, scores, peak):
        wide = jnp.concatenate([peak] * (scores.shape[1] // self.width), 1)
        return jnp.exp2((scores - wide) * self.factor).astype(BF16)

    def mixed(self, g, probs, picks):
        tokens = self.tokens
        rows = pl.ds((self.kv_heads + g) * tokens, tokens)
        values = jnp.concatenate([ref[slot, rows, :] for ref, slot in picks], 0)
        return dot(probs, jnp.concatenate([values, jnp.ones_like(values)], 1), ((1,), (0,)))

    def top(self, scores):
        return jnp.broadcast_to(jnp.max(scores, axis=1, keepdims=True), (scores.shape[0], self.width))

    def added(self, own, g, marks, picks, sums, before):
        scores = self.scores(own, g, marks, picks)
        peak = jnp.maximum(before, self.top(scores))
        scale = jnp.exp2((before - peak) * self.factor)
        out = self.mixed(g, self.probs(scores, peak), picks) + sums * jnp.concatenate([scale, scale], 1)
        return out, peak


def home_kernel(places, share, at_ref, got_ref, query_ref, home_ref, sums_ref, peaks_ref, marks_ref, codes, fills):
    soft = Soft(places, at_ref, query_ref, got_ref, home_ref, share, codes)
    row_at = lax.broadcasted_iota(jnp.int32, soft.lane.shape, 0)
    fills[...] = soft.spread(jnp.where(row_at >= soft.lane, 0.0, NEG_FILL))
    for own in range(LOOK):
        block = soft.core if own else 1 - soft.core
        mine = (home_ref, 2 * block)
        picks = [(home_ref, 1 - block), (home_ref, 3), mine]
        soft.code(own, picks)
        marks_ref[own] = soft.spread(jnp.where(soft.marked(mine), 0.0, NEG_FILL)).astype(BF16)
        last = (len(picks) - 1) * soft.tokens
        for g in range(soft.kv_heads):
            scores = soft.scores(own, g, marks_ref[own], picks)
            scores = jnp.concatenate([scores[:, :last], scores[:, last:] + fills[...]], 1)
            peak = soft.top(scores)
            at = own * soft.kv_heads + g
            sums_ref[at] = soft.mixed(g, soft.probs(scores, peak), picks)
            peaks_ref[at] = peak


def away_kernel(places, share, at_ref, got_ref, query_ref, home_ref, sums_ref, peaks_ref, marks_ref, *rest):
    pays, outs, codes = rest[: places - 1], rest[places - 1 : places + 1], rest[places + 1]
    soft = Soft(places, at_ref, query_ref, got_ref, home_ref, share, codes)
    for own in range(LOOK):
        picks = soft.far(soft.core if own else 1 - soft.core, range(1, places), pays)
        soft.code(own, picks)
        mixed = []
        for g in range(soft.kv_heads):
            at = own * soft.kv_heads + g
            out, _ = soft.added(own, g, marks_ref[own], picks, sums_ref[at], peaks_ref[at])
            mixed.append((out[:, : soft.width] / out[:, soft.width :]).reshape(soft.tokens, share, soft.width))
        outs[own][...] = jnp.concatenate(mixed, 1).astype(BF16)


def body(
    light_query,
    light_keys,
    light_values,
    decay_rate,
    norm_gain,
    soft_query,
    soft_keys,
    soft_values,
    segment_ids,
):
    places = lax.axis_size("head")
    n_all = lax.axis_size("ctx") * places
    members = LOOK * places
    core = lax.rem(lax.axis_index("ctx"), LOOK)
    place = lax.axis_index("head")
    at = jnp.stack([core, place, core * places + place]).astype(jnp.int32)
    tokens, heads, width = light_query.shape
    kv_heads = soft_keys.shape[1]
    per, half, kv_half = heads // places, heads // LOOK, kv_heads // LOOK
    sid_row = segment_ids.reshape(1, tokens)
    even, uneven = [k for k in range(places) if not odd(k)], [k for k in range(places) if odd(k)]

    def partner(value, k):
        pairs = [(i, i - i % members + ((i % members) ^ k)) for i in range(n_all)]
        return lax.ppermute(value, AXES, pairs)

    def across(value):
        return partner(value, places)

    def to_places(values):
        return [values[0]] + [partner(values[k], k) for k in range(1, places)]

    def onward(value, groups):
        step = groups * places
        return lax.ppermute(value, AXES, [(i, i + step) for i in range(n_all - step)])

    def shape(*dims):
        return jax.ShapeDtypeStruct(dims, BF16)

    def room(*dims, dtype=BF16):
        return pltpu.VMEM(dims, dtype)

    def semaphores(count):
        return pltpu.SemaphoreType.DMA((count,))

    pay = shape(2 * kv_half * tokens + TAIL, width)
    pair = shape(LOOK * (pay.shape[0] - TAIL) + TAIL, width)
    given = shape(pay.shape[0] // half + tokens, half, width)
    state = shape(per * width + TAIL, width)
    by_head = shape(heads, tokens, width)
    half_out = shape(tokens, half, width)
    slots = room(places, *state.shape)
    sid_room = room(1, tokens, dtype=jnp.int32)

    def held(value):
        return pltpu.with_memory_space_constraint(value, pltpu.HBM)

    made = call(
        functools.partial(source_kernel, places), "source", 0, 16, [SMEM] + [HBM] * 7,
        [shape(state.shape[0] + TAIL, width)] * places + [by_head] * 2 + [pair, given], [VMEM] * (places + 4),
        [pltpu.SMEM((heads,), F32), sid_room] + [room(tokens, heads, width)] * 2 + [room(tokens, kv_heads, width)] * 2
        + [room(kv_heads, tokens, width), semaphores(7)],
    )(at, *[held(x) for x in (decay_rate, sid_row, light_keys, light_values, soft_keys, soft_values, soft_query)])
    keys_by_head, values_by_head, own, give = made[places:]
    states = to_places(made[:places])
    got = across(give)
    own = call(pair_kernel, "pair", 0, 8, [SMEM, VMEM, VMEM], pair, VMEM, aliases={2: 0})(at, got, own)
    before = onward(own, LOOK)

    left = call(
        prep_kernel, "prep", 0, 16, [SMEM, VMEM, VMEM, VMEM], shape(heads, tokens, tokens + width), VMEM
    )(decay_rate, sid_row, light_query, keys_by_head)
    mixed = call(
        functools.partial(mix_kernel, places), "mix", 0, 8, [SMEM] + [VMEM] * 2,
        [shape(4, *pay.shape)] + [shape(3, *pay.shape)] * (places - 1), [VMEM] * places, after=[left, *[states[k] for k in even[1:]]],
    )(at, own, before)
    home = mixed[0]
    parcels = to_places(mixed)

    ending = call(
        functools.partial(ending_kernel, places, tokens), "ending", 0, 8, [SMEM] * 2 + [VMEM] * places, state, VMEM,
        [slots], after=[home],
    )(at, decay_rate, *states)
    ahead = [onward(ending, groups) for groups in range(1, LOOK + 1)]
    share = half // kv_half
    queries = tokens * share

    def codes(blocks):
        return room(LOOK, blocks * tokens, width)

    def limit(blocks):
        return (blocks * tokens * queries * 14 + 8 * half_out.size) / 2**20 + 8

    sums_like = [
        jax.ShapeDtypeStruct((LOOK * kv_half, queries, 2 * width), F32),
        jax.ShapeDtypeStruct((LOOK * kv_half, queries, width), F32),
    ]
    sums, peaks, marks = call(
        functools.partial(home_kernel, places, share), "home", 0, limit(3), [SMEM] + [VMEM] * 3,
        sums_like + [shape(LOOK, queries, tokens)], [VMEM] * 3, [codes(3), room(queries, tokens, dtype=F32)], after=[ending],
    )(at, got, soft_query, home)
    prefixed = call(
        functools.partial(prefix_kernel, places, tokens), "prefix", 0, 12, [SMEM] * 2 + [VMEM] * (places + LOOK),
        [state] * places, [VMEM] * places, [slots, slots], after=[sums],
    )(at, decay_rate, *ahead, *states)
    entries = to_places(prefixed)

    blocks = 2 * (places - 1)
    soft_theirs, soft_kept = call(
        functools.partial(away_kernel, places, share), "away", 30, limit(blocks), [SMEM] + [VMEM] * (5 + places),
        [half_out] * 2, [VMEM] * 2, [codes(blocks)], after=[prefixed[0]],
    )(at, got, soft_query, home, sums, peaks, marks, *parcels[1:])

    whole = shape(tokens, heads, width)
    known = (at, decay_rate, sid_row, norm_gain, left, values_by_head)
    rooms = [room(half, tokens, width), room(tokens, half, width)]
    light_out, soft_out, soft_theirs = call(
        functools.partial(first_kernel, places, even), "first", 0, 16, [SMEM] * 2 + [VMEM] * 5 + [ANY] + [VMEM] * len(even),
        [whole, whole, half_out], [HBM, HBM, ANY], rooms + [semaphores(2)], aliases={7: 2},
    )(*known, soft_kept, soft_theirs, *[entries[k] for k in even])
    soft_got = across(soft_theirs)
    light_out, done = call(
        functools.partial(second_kernel, places, uneven), "second", 15, 16, [SMEM] * 2 + [VMEM] * 4 + [HBM] + [VMEM] * len(uneven),
        [whole, shape(TAIL, width)], [HBM, VMEM], rooms + [semaphores(1)], aliases={6: 0},
    )(*known, light_out, *[entries[k] for k in uneven])
    soft_out = call(
        beside_kernel, "beside", 0, 8, [SMEM, VMEM, HBM], whole, HBM, [semaphores(math.gcd(tokens, 4))], aliases={2: 0}, after=[done]
    )(at, soft_got, soft_out)
    return (light_out, soft_out)


def solution(mesh):
    placed = P(("ctx", "head"), None, None)
    return jax.shard_map(
        body,
        mesh=mesh,
        in_specs=(placed, placed, placed, P(), P(), placed, placed, placed, P(("ctx", "head"))),
        out_specs=(placed, placed),
        check_vma=False,
    )
```

```python
import functools
import math

import jax
import jax.numpy as jnp
from jax import lax
from jax.experimental import pallas as pl
from jax.experimental.pallas import tpu as pltpu
from jax.sharding import PartitionSpec as P

LOOK = 2
PARTS = 2
PIECES = 4
NEG_FILL = -1e30
NORM_EPS = 1e-06
TAIL = 16
F32 = jnp.float32
BF16 = jnp.bfloat16
AXES = ("ctx", "head")
VMEM = pl.BlockSpec(memory_space=pltpu.VMEM)
SMEM = pl.BlockSpec(memory_space=pltpu.SMEM)
ANY = pl.BlockSpec(memory_space=pl.ANY)
HBM = pl.BlockSpec(memory_space=pltpu.HBM)


def call(kernel, name, micros, limit_mib, ins, outs, out_specs, scratch=(), aliases=None, after=()):
    count = len(ins)

    def run(*refs):
        kernel(*refs[:count], *refs[count + len(after) :])

    made = pl.pallas_call(
        run,
        out_shape=outs,
        in_specs=list(ins) + [ANY] * len(after),
        out_specs=out_specs,
        scratch_shapes=list(scratch),
        input_output_aliases=aliases or {},
        compiler_params=pltpu.CompilerParams(vmem_limit_bytes=int(limit_mib * 1024 * 1024)),
        cost_estimate=pl.CostEstimate(flops=int(micros * 1e9), bytes_accessed=0, transcendentals=0),
        name=name,
    )
    return lambda *args: made(*args, *after)


def column(row):
    size = row.shape[1]
    return jnp.transpose(jnp.broadcast_to(row, (size, size)))


def dot(left, right, contract):
    return lax.dot_general(left, right, (contract, ((), ())), preferred_element_type=F32)


def odd(place):
    for shift in (8, 4, 2, 1):
        place = place ^ (place >> shift)
    return place & 1


def share_of(places, place):
    return odd(place) * (places // 2) + (place >> 1)


def pieces(tokens):
    return [pl.ds(n * (tokens // PIECES), tokens // PIECES) for n in range(PIECES)]


def copy_out(stage, hbm, columns, sems):
    copies = [
        pltpu.make_async_copy(stage.at[piece], hbm.at[piece, columns, :], sems.at[n])
        for n, piece in enumerate(pieces(stage.shape[0]))
    ]
    for copy in copies:
        copy.start()
    return copies


def split(value):
    high = value.astype(BF16)
    return high, (value - high.astype(F32)).astype(BF16)


def source_kernel(places, at_ref, rate_hbm, sid_hbm, key_hbm, value_hbm, soft_key_hbm, soft_value_hbm, soft_query_hbm, *rest):
    outs, rest = rest[:places], rest[places:]
    keys_by_head, values_by_head, pair_ref, give_ref, rate_ref, sid_ref, key_in, value_in, soft_key_in, soft_value_in, stage, sems = rest
    heads, tokens, width = keys_by_head.shape
    per, half = heads // places, heads // LOOK
    kv_heads = soft_key_in.shape[1]
    kv_half = kv_heads // LOOK
    span = 2 * kv_half * tokens
    rows = span + TAIL
    core, place = at_ref[0], at_ref[1]
    mine = pl.multiple_of(core * span, TAIL)
    theirs = pl.ds(pl.multiple_of((LOOK - 1 - core) * half, half), half)
    moves = (
        (soft_key_hbm, soft_key_in),
        (soft_value_hbm, soft_value_in),
        (sid_hbm, sid_ref),
        (rate_hbm, rate_ref),
        *[(hbm.at[piece], ref.at[piece]) for piece in pieces(tokens) for hbm, ref in ((key_hbm, key_in), (value_hbm, value_in))],
        (soft_query_hbm.at[:, theirs, :], give_ref.at[pl.ds(rows // half, tokens)]),
    )
    copies = [pltpu.make_async_copy(src, dst, sems.at[n]) for n, (src, dst) in enumerate(moves)]
    for copy in copies:
        copy.start()
    for at, ref in enumerate((soft_key_in, soft_value_in)):
        copies[at].wait()
        stage[...] = jnp.swapaxes(ref[...], 0, 1)
        for j in range(kv_half):
            start = (at * kv_half + j) * tokens
            pair_ref[pl.ds(mine + start, tokens), :] = stage[core * kv_half + j]
            block = stage[(LOOK - 1 - core) * kv_half + j]
            give_ref[pl.ds(start // half, tokens // half)] = block.reshape(tokens // half, half, width)
    copies[2].wait()
    sid_row = (sid_ref[...] + 1).astype(F32)
    tail = jnp.broadcast_to(sid_row, (TAIL, tokens)).astype(BF16)
    pair_ref[pl.ds(LOOK * span, TAIL), :] = tail
    give_ref[pl.ds(2 * kv_half * tokens // half, TAIL // half)] = tail.reshape(TAIL // half, half, tokens)
    open_row = (sid_row == jnp.max(sid_row, axis=1, keepdims=True)).astype(F32)
    behind = (tokens - 1 - lax.broadcasted_iota(jnp.int32, (1, tokens), 1)).astype(F32)
    copies[3].wait()
    for n, piece in enumerate(pieces(tokens)):
        copies[4 + 2 * n].wait()
        keys_by_head[:, piece, :] = jnp.swapaxes(key_in[piece], 0, 1)
        copies[5 + 2 * n].wait()
        values_by_head[:, piece, :] = jnp.swapaxes(value_in[piece], 0, 1)
    for k in range(places):
        for j in range(per):
            head = share_of(places, place ^ k) * per + j
            values = values_by_head[head]
            weighted = jnp.transpose(keys_by_head[head].astype(F32)) * (open_row * jnp.exp(-rate_ref[head] * behind))
            high, low = split(weighted)
            state = dot(jnp.concatenate([high, low], 1), jnp.concatenate([values, values], 0), ((1,), (0,)))
            outs[k][pl.ds(j * width, width), :] = state.astype(BF16)
        outs[k][pl.ds(per * width, TAIL), :] = tail
        outs[k][pl.ds(per * width + TAIL, TAIL), :] = tail
    copies[-1].wait()


def pair_kernel(at_ref, got_ref, _, pair_ref):
    heads = got_ref.shape[1]
    width = pair_ref.shape[1]
    span = (pair_ref.shape[0] - TAIL) // LOOK
    other = 1 - at_ref[0]
    pair_ref[pl.ds(pl.multiple_of(other * span, TAIL), span), :] = got_ref[pl.ds(0, span // heads)].reshape(span, width)
    theirs = got_ref[pl.ds(span // heads, TAIL // heads)].reshape(TAIL, width)
    row_at = lax.broadcasted_iota(jnp.int32, (TAIL, width), 0)
    mine = pair_ref[pl.ds(LOOK * span, TAIL), :].astype(F32)
    tail = jnp.where(row_at // (TAIL // LOOK) == other, theirs.astype(F32), mine)
    pair_ref[pl.ds(LOOK * span, TAIL), :] = tail.astype(BF16)


def mix_kernel(places, at_ref, pair_ref, before_ref, *rest):
    home_ref, outs = rest[-places], rest[1 - places :]
    width = pair_ref.shape[1]
    span = (pair_ref.shape[0] - TAIL) // LOOK
    place = at_ref[1]
    for back, ref in enumerate((pair_ref, before_ref)):
        tails = ref[pl.ds(LOOK * span, TAIL), :].astype(F32)
        for block in range(LOOK):
            slot = LOOK * block + back
            home_ref[slot, pl.ds(0, span), :] = ref[pl.ds(block * span, span), :]
            row = block * (TAIL // LOOK)
            home_ref[slot, pl.ds(span, TAIL), :] = jnp.broadcast_to(tails[row : row + 1], (TAIL, width)).astype(BF16)
    for k in range(1, places):
        out = outs[k - 1]
        later = ((place ^ k) > place).astype(jnp.int32)
        out[0] = home_ref[0]
        out[1] = home_ref[3]
        out[2] = home_ref[1 + later]


def gather_slots(places, at_ref, pays, slots):
    for k in range(places):
        slots[at_ref[1] ^ k] = pays[k][pl.ds(0, slots.shape[1]), :]


def last_of(pay, per, width):
    return jnp.max(pay[pl.ds(per * width, TAIL), :].astype(F32), axis=(0, 1), keepdims=True)


def advance(pay, per, width, span, rates, state, last):
    now = last_of(pay, per, width)
    same = (now == last).astype(F32)
    state = [
        pay[pl.ds(j * width, width), :].astype(F32) + (same * jnp.exp(jnp.full((1, width), -rates[j] * span, F32))) * state[j]
        for j in range(per)
    ]
    return state, now


def store_state(ref, state, last):
    width = ref.shape[1]
    for j, value in enumerate(state):
        ref[pl.ds(j * width, width), :] = value.astype(BF16)
    tail = ref.shape[0] - len(state) * width
    ref[pl.ds(len(state) * width, tail), :] = jnp.broadcast_to(last, (tail, width)).astype(BF16)


def ending_kernel(places, tokens, at_ref, rate_ref, *rest):
    pays, outs, slots = rest[:places], rest[places : places + LOOK], rest[places + LOOK]
    width = outs[0].shape[1]
    per = (outs[0].shape[0] - TAIL) // width
    gather_slots(places, at_ref, pays, slots)
    rates = [rate_ref[share_of(places, at_ref[1]) * per + j] for j in range(per)]
    state = [jnp.zeros((width, width), F32)] * per
    last = jnp.zeros((1, 1), F32)
    for block in range(places):
        state, last = advance(slots.at[block], per, width, tokens, rates, state, last)
    for out_ref in outs:
        store_state(out_ref, state, last)


def prefix_kernel(places, tokens, at_ref, rate_ref, *rest):
    ahead, pays, outs = rest[:LOOK], rest[LOOK : LOOK + places], rest[LOOK + places : LOOK + 2 * places]
    slots, results = rest[LOOK + 2 * places :]
    width = ahead[0].shape[1]
    per = (ahead[0].shape[0] - TAIL) // width
    gather_slots(places, at_ref, pays, slots)
    rates = [rate_ref[share_of(places, at_ref[1]) * per + j] for j in range(per)]
    state = [ahead[-1][pl.ds(j * width, width), :].astype(F32) for j in range(per)]
    last = last_of(ahead[-1], per, width)
    for group in reversed(ahead[:-1]):
        state, last = advance(group, per, width, places * tokens, rates, state, last)
    for block in range(places):
        store_state(results.at[block], state, last)
        if block < places - 1:
            state, last = advance(slots.at[block], per, width, tokens, rates, state, last)
    for k in range(places):
        outs[k][...] = results[at_ref[1] ^ k]


def prep_kernel(rate_ref, sid_ref, query_ref, keys_by_head, left_ref):
    heads, tokens, _ = keys_by_head.shape
    sid_row = (sid_ref[...] + 1).astype(F32)
    row_at = lax.broadcasted_iota(jnp.int32, (tokens, tokens), 0)
    lane = lax.broadcasted_iota(jnp.int32, (tokens, tokens), 1)
    allowed = ((row_at >= lane) & (column(sid_row) == sid_row)).astype(F32)
    ahead = (lax.broadcasted_iota(jnp.int32, (1, tokens), 1) + 1).astype(F32)
    left_ref[:, :, tokens:] = jnp.swapaxes(query_ref[...], 0, 1)
    for head in range(heads):
        weights = dot(left_ref[head, :, tokens:], keys_by_head[head], ((1,), (1,)))
        weights = weights * allowed * jnp.exp(rate_ref[head] * ahead)
        left_ref[head, :, :tokens] = weights.astype(BF16)


class Light:
    def __init__(self, places, at_ref, rate_ref, sid_ref, gain_ref, left_ref, values_by_head, pay):
        self.rate_ref, self.gain_ref, self.left_ref, self.values_by_head = rate_ref, gain_ref, left_ref, values_by_head
        heads, self.tokens, self.width = values_by_head.shape
        self.places, self.place, self.core = places, at_ref[1], at_ref[0]
        self.half, self.per = heads // LOOK, heads // places
        sid_column = column((sid_ref[...] + 1).astype(F32))
        self.continues = (sid_column == last_of(pay, self.per, self.width)).astype(BF16)
        self.ahead = (lax.broadcasted_iota(jnp.int32, (self.tokens, 1), 0) + 1).astype(F32)

    def columns(self, which):
        return pl.ds(pl.multiple_of(which * self.half, self.half), self.half)

    def half_out(self, ks, pays, light_hbm, by_head, stage, sems):
        which = odd(self.place ^ ks[0])
        for k, pay in zip(ks, pays):
            for j in range(self.per):
                head = share_of(self.places, self.place ^ k) * self.per + j
                tokens = self.tokens
                left = jnp.concatenate([self.left_ref[head, :, :tokens], self.left_ref[head, :, tokens:] * self.continues], 1)
                right = jnp.concatenate([self.values_by_head[head], pay[pl.ds(j * self.width, self.width), :]], 0)
                raw = dot(left, right, ((1,), (0,)))
                lead = jnp.exp(-self.rate_ref[head] * self.ahead)
                mean_square = jnp.mean(raw * raw, axis=1, keepdims=True) * (lead * lead)
                out = raw * (lead * lax.rsqrt(mean_square + NORM_EPS)) * self.gain_ref[pl.ds(head, 1), :]
                by_head[head - which * self.half] = out.astype(BF16)
        stage[...] = jnp.swapaxes(by_head[...], 0, 1)
        for copy in copy_out(stage, light_hbm, self.columns(which), sems):
            copy.wait()


def first_kernel(places, ks, at_ref, rate_ref, sid_ref, gain_ref, left_ref, values_by_head, keep_ref, *rest):
    pays, rest = rest[PARTS : PARTS + len(ks)], rest[PARTS + len(ks) :]
    light_hbm, soft_hbm, (by_head, stage, sems) = rest[0], rest[1], rest[2 + PARTS :]
    light = Light(places, at_ref, rate_ref, sid_ref, gain_ref, left_ref, values_by_head, pays[0])
    copy = pltpu.make_async_copy(keep_ref, soft_hbm.at[:, light.columns(light.core), :], sems.at[0])
    copy.start()
    light.half_out(ks, pays, light_hbm, by_head, stage, sems.at[pl.ds(1, PIECES)])
    copy.wait()


def second_kernel(places, ks, at_ref, rate_ref, sid_ref, gain_ref, left_ref, values_by_head, *rest):
    got, rest = rest[:PARTS], rest[PARTS + 2 :]
    pays, (light_hbm, soft_hbm, by_head, stage, sems) = rest[: len(ks)], rest[len(ks) :]
    light = Light(places, at_ref, rate_ref, sid_ref, gain_ref, left_ref, values_by_head, pays[0])
    size = light.tokens // PARTS
    copies = []
    for n in range(PARTS):
        there = soft_hbm.at[pl.ds(n * size, size), light.columns(LOOK - 1 - light.core), :]
        copies.append(pltpu.make_async_copy(got[n], there, sems.at[PIECES + n]))
        copies[-1].start()
    light.half_out(ks, pays, light_hbm, by_head, stage, sems)
    for copy in copies:
        copy.wait()


class Soft:
    def __init__(self, places, at_ref, query_ref, got_ref, home_ref, share, codes):
        self.core, self.place = at_ref[0], at_ref[1]
        self.tokens, _, self.width = query_ref.shape
        self.share, self.heads, self.rows = share, got_ref.shape[1], home_ref.shape[1]
        self.kv_heads = self.heads // share
        self.query_ref, self.got_ref, self.codes = query_ref, got_ref, codes
        self.lane = lax.broadcasted_iota(jnp.int32, (self.tokens, self.tokens), 1)
        self.factor = self.width ** (-0.5) * math.log2(math.e)

    def spread(self, value):
        tokens, share = self.tokens, self.share
        value = jnp.broadcast_to(value.reshape(tokens, 1, tokens), (tokens, share, tokens))
        return value.reshape(tokens * share, tokens)

    def marked(self, pick):
        ref, slot = pick
        sids = ref[slot, pl.ds(2 * self.kv_heads * self.tokens, TAIL), :].astype(F32)[0:1, :]
        return column(sids) == self.lane.astype(F32)

    def far(self, block, ks, pays):
        picks = []
        for k, pay in zip(ks, pays):
            later = ((self.place ^ k) > self.place).astype(jnp.int32)
            picks.append((pay, 2 * later * (1 - block)))
            picks.append((pay, 1 + (1 - later) * block))
        return picks

    def code(self, own, picks):
        for at, pick in enumerate(picks):
            self.codes[own, pl.ds(at * self.tokens, self.tokens), :] = self.marked(pick).astype(BF16)

    def query(self, own, g):
        tokens, share = self.tokens, self.share
        if own:
            first = pl.multiple_of(self.core * self.heads, self.heads)
            wide = self.query_ref[:, pl.ds(first, self.heads), :]
        else:
            wide = self.got_ref[pl.ds(self.rows // self.heads, tokens)]
        wide = wide.astype(F32)[:, g * share : (g + 1) * share, :]
        return wide.reshape(tokens * share, self.width).astype(BF16)

    def scores(self, own, g, marks, picks):
        tokens = self.tokens
        query = jnp.concatenate([self.query(own, g), marks], 1)
        keys = jnp.concatenate([ref[slot, pl.ds(g * tokens, tokens), :] for ref, slot in picks], 0)
        codes = self.codes[own, pl.ds(0, len(picks) * tokens), :]
        return dot(query, jnp.concatenate([keys, codes], 1), ((1,), (1,)))

    def probs(self, scores, peak):
        wide = jnp.concatenate([peak] * (scores.shape[1] // self.width), 1)
        return jnp.exp2((scores - wide) * self.factor).astype(BF16)

    def mixed(self, g, probs, picks):
        tokens = self.tokens
        rows = pl.ds((self.kv_heads + g) * tokens, tokens)
        values = jnp.concatenate([ref[slot, rows, :] for ref, slot in picks], 0)
        return dot(probs, jnp.concatenate([values, jnp.ones_like(values)], 1), ((1,), (0,)))

    def top(self, scores):
        return jnp.broadcast_to(jnp.max(scores, axis=1, keepdims=True), (scores.shape[0], self.width))

    def added(self, own, g, marks, picks, sums, before):
        scores = self.scores(own, g, marks, picks)
        peak = jnp.maximum(before, self.top(scores))
        scale = jnp.exp2((before - peak) * self.factor)
        out = self.mixed(g, self.probs(scores, peak), picks) + sums * jnp.concatenate([scale, scale], 1)
        return out, peak


def home_kernel(places, share, at_ref, got_ref, query_ref, home_ref, sums_ref, peaks_ref, marks_ref, codes, fills):
    soft = Soft(places, at_ref, query_ref, got_ref, home_ref, share, codes)
    row_at = lax.broadcasted_iota(jnp.int32, soft.lane.shape, 0)
    fills[...] = soft.spread(jnp.where(row_at >= soft.lane, 0.0, NEG_FILL))
    for own in range(LOOK):
        block = soft.core if own else 1 - soft.core
        mine = (home_ref, 2 * block)
        picks = [(home_ref, 1 - block), (home_ref, 3), mine]
        soft.code(own, picks)
        marks_ref[own] = soft.spread(jnp.where(soft.marked(mine), 0.0, NEG_FILL)).astype(BF16)
        last = (len(picks) - 1) * soft.tokens
        for g in range(soft.kv_heads):
            scores = soft.scores(own, g, marks_ref[own], picks)
            scores = jnp.concatenate([scores[:, :last], scores[:, last:] + fills[...]], 1)
            peak = soft.top(scores)
            at = own * soft.kv_heads + g
            sums_ref[at] = soft.mixed(g, soft.probs(scores, peak), picks)
            peaks_ref[at] = peak


def away_kernel(places, share, at_ref, got_ref, query_ref, home_ref, sums_ref, peaks_ref, marks_ref, *rest):
    pays, rest = rest[: places - 1], rest[places - 1 :]
    given, kept, codes = rest[:PARTS], rest[PARTS], rest[PARTS + 1]
    soft = Soft(places, at_ref, query_ref, got_ref, home_ref, share, codes)
    for own in range(LOOK):
        picks = soft.far(soft.core if own else 1 - soft.core, range(1, places), pays)
        soft.code(own, picks)
        mixed = []
        for g in range(soft.kv_heads):
            at = own * soft.kv_heads + g
            out, _ = soft.added(own, g, marks_ref[own], picks, sums_ref[at], peaks_ref[at])
            mixed.append((out[:, : soft.width] / out[:, soft.width :]).reshape(soft.tokens, share, soft.width))
        mixed = jnp.concatenate(mixed, 1).astype(BF16)
        if own:
            kept[...] = mixed
        else:
            size = soft.tokens // PARTS
            for n in range(PARTS):
                given[n][...] = mixed[n * size : (n + 1) * size]


def body(
    light_query,
    light_keys,
    light_values,
    decay_rate,
    norm_gain,
    soft_query,
    soft_keys,
    soft_values,
    segment_ids,
):
    places = lax.axis_size("head")
    n_all = lax.axis_size("ctx") * places
    members = LOOK * places
    core = lax.rem(lax.axis_index("ctx"), LOOK)
    place = lax.axis_index("head")
    at = jnp.stack([core, place, core * places + place]).astype(jnp.int32)
    tokens, heads, width = light_query.shape
    kv_heads = soft_keys.shape[1]
    per, half, kv_half = heads // places, heads // LOOK, kv_heads // LOOK
    sid_row = segment_ids.reshape(1, tokens)
    even, uneven = [k for k in range(places) if not odd(k)], [k for k in range(places) if odd(k)]

    def partner(value, k):
        pairs = [(i, i - i % members + ((i % members) ^ k)) for i in range(n_all)]
        return lax.ppermute(value, AXES, pairs)

    def across(value):
        return partner(value, places)

    def to_places(values):
        return [values[0]] + [partner(values[k], k) for k in range(1, places)]

    def onward(value, groups):
        step = groups * places
        return lax.ppermute(value, AXES, [(i, i + step) for i in range(n_all - step)])

    def shape(*dims):
        return jax.ShapeDtypeStruct(dims, BF16)

    def room(*dims, dtype=BF16):
        return pltpu.VMEM(dims, dtype)

    def semaphores(count):
        return pltpu.SemaphoreType.DMA((count,))

    pay = shape(2 * kv_half * tokens + TAIL, width)
    pair = shape(LOOK * (pay.shape[0] - TAIL) + TAIL, width)
    given = shape(pay.shape[0] // half + tokens, half, width)
    state = shape(per * width + TAIL, width)
    by_head = shape(heads, tokens, width)
    half_out = shape(tokens, half, width)
    slots = room(places, *state.shape)
    sid_room = room(1, tokens, dtype=jnp.int32)

    def held(value):
        return pltpu.with_memory_space_constraint(value, pltpu.HBM)

    made = call(
        functools.partial(source_kernel, places), "source", 0, 16, [SMEM] + [HBM] * 7,
        [shape(state.shape[0] + TAIL, width)] * places + [by_head] * 2 + [pair, given], [VMEM] * (places + 4),
        [pltpu.SMEM((heads,), F32), sid_room] + [room(tokens, heads, width)] * 2 + [room(tokens, kv_heads, width)] * 2
        + [room(kv_heads, tokens, width), semaphores(5 + 2 * PIECES)],
    )(at, *[held(x) for x in (decay_rate, sid_row, light_keys, light_values, soft_keys, soft_values, soft_query)])
    keys_by_head, values_by_head, own, give = made[places:]
    states = to_places(made[:places])
    got = across(give)
    own = call(pair_kernel, "pair", 0, 8, [SMEM, VMEM, VMEM], pair, VMEM, aliases={2: 0})(at, got, own)
    before = onward(own, LOOK)

    left = call(
        prep_kernel, "prep", 0, 16, [SMEM, VMEM, VMEM, VMEM], shape(heads, tokens, tokens + width), VMEM
    )(decay_rate, sid_row, light_query, keys_by_head)
    mixed = call(
        functools.partial(mix_kernel, places), "mix", 0, 8, [SMEM] + [VMEM] * 2,
        [shape(4, *pay.shape)] + [shape(3, *pay.shape)] * (places - 1), [VMEM] * places, after=[left, *[states[k] for k in even[1:]]],
    )(at, own, before)
    home = mixed[0]
    parcels = to_places(mixed)

    ending = call(
        functools.partial(ending_kernel, places, tokens), "ending", 0, 8, [SMEM] * 2 + [VMEM] * places,
        [state] * LOOK, [VMEM] * LOOK, [slots], after=[home],
    )(at, decay_rate, *states)
    ahead = [onward(ending[n], n + 1) for n in range(LOOK)]
    share = half // kv_half
    queries = tokens * share

    def codes(blocks):
        return room(LOOK, blocks * tokens, width)

    def limit(blocks):
        return (blocks * tokens * queries * 14 + 8 * half_out.size) / 2**20 + 8

    sums_like = [
        jax.ShapeDtypeStruct((LOOK * kv_half, queries, 2 * width), F32),
        jax.ShapeDtypeStruct((LOOK * kv_half, queries, width), F32),
    ]
    sums, peaks, marks = call(
        functools.partial(home_kernel, places, share), "home", 0, limit(3), [SMEM] + [VMEM] * 3,
        sums_like + [shape(LOOK, queries, tokens)], [VMEM] * 3, [codes(3), room(queries, tokens, dtype=F32)], after=[ending[0]],
    )(at, got, soft_query, home)
    prefixed = call(
        functools.partial(prefix_kernel, places, tokens), "prefix", 0, 12, [SMEM] * 2 + [VMEM] * (places + LOOK),
        [state] * places, [VMEM] * places, [slots, slots], after=[sums],
    )(at, decay_rate, *ahead, *states)
    entries = to_places(prefixed)

    blocks = 2 * (places - 1)
    part_out = shape(tokens // PARTS, half, width)
    made = call(
        functools.partial(away_kernel, places, share), "away", 30, limit(blocks), [SMEM] + [VMEM] * (5 + places),
        [part_out] * PARTS + [half_out], [VMEM] * (PARTS + 1), [codes(blocks)], after=[prefixed[0]],
    )(at, got, soft_query, home, sums, peaks, marks, *parcels[1:])
    soft_theirs, soft_kept = made[:PARTS], made[PARTS]

    whole = shape(tokens, heads, width)
    known = (at, decay_rate, sid_row, norm_gain, left, values_by_head)
    rooms = [room(half, tokens, width), room(tokens, half, width)]
    made = call(
        functools.partial(first_kernel, places, even), "first", 0, 16,
        [SMEM] * 2 + [VMEM] * 5 + [ANY] * PARTS + [VMEM] * len(even), [whole, whole] + [part_out] * PARTS, [HBM, HBM] + [ANY] * PARTS,
        rooms + [semaphores(1 + PIECES)], aliases={7 + n: 2 + n for n in range(PARTS)},
    )(*known, soft_kept, *soft_theirs, *[entries[k] for k in even])
    soft_got = [across(x) for x in made[2:]]
    return tuple(
        call(
            functools.partial(second_kernel, places, uneven), "second", 15, 16,
            [SMEM] * 2 + [VMEM] * (4 + PARTS) + [HBM] * 2 + [VMEM] * len(uneven), [whole, whole], [HBM, HBM],
            rooms + [semaphores(PIECES + PARTS)], aliases={6 + PARTS: 0, 7 + PARTS: 1},
        )(*known, *soft_got, made[0], made[1], *[entries[k] for k in uneven])
    )


def solution(mesh):
    placed = P(("ctx", "head"), None, None)
    return jax.shard_map(
        body,
        mesh=mesh,
        in_specs=(placed, placed, placed, P(), P(), placed, placed, placed, P(("ctx", "head"))),
        out_specs=(placed, placed),
        check_vma=False,
    )
```

```python
import functools
import math

import jax
import jax.numpy as jnp
from jax import lax
from jax.experimental import pallas as pl
from jax.experimental.pallas import tpu as pltpu
from jax.sharding import PartitionSpec as P

LOOK = 2
PARTS = 2
PIECES = 4
NEG_FILL = -1e30
NORM_EPS = 1e-06
TAIL = 16
F32 = jnp.float32
BF16 = jnp.bfloat16
AXES = ("ctx", "head")
VMEM = pl.BlockSpec(memory_space=pltpu.VMEM)
SMEM = pl.BlockSpec(memory_space=pltpu.SMEM)
ANY = pl.BlockSpec(memory_space=pl.ANY)
HBM = pl.BlockSpec(memory_space=pltpu.HBM)


def call(kernel, name, micros, limit_mib, ins, outs, out_specs, scratch=(), aliases=None, after=()):
    count = len(ins)

    def run(*refs):
        kernel(*refs[:count], *refs[count + len(after) :])

    made = pl.pallas_call(
        run,
        out_shape=outs,
        in_specs=list(ins) + [ANY] * len(after),
        out_specs=out_specs,
        scratch_shapes=list(scratch),
        input_output_aliases=aliases or {},
        compiler_params=pltpu.CompilerParams(vmem_limit_bytes=int(limit_mib * 1024 * 1024)),
        cost_estimate=pl.CostEstimate(flops=int(micros * 1e9), bytes_accessed=0, transcendentals=0),
        name=name,
    )
    return lambda *args: made(*args, *after)


def column(row):
    size = row.shape[1]
    return jnp.transpose(jnp.broadcast_to(row, (size, size)))


def dot(left, right, contract):
    return lax.dot_general(left, right, (contract, ((), ())), preferred_element_type=F32)


def odd(place):
    for shift in (8, 4, 2, 1):
        place = place ^ (place >> shift)
    return place & 1


def share_of(places, place):
    return odd(place) * (places // 2) + (place >> 1)


def pieces(tokens):
    return [pl.ds(n * (tokens // PIECES), tokens // PIECES) for n in range(PIECES)]


def copy_out(stage, hbm, columns, sems):
    copies = [
        pltpu.make_async_copy(stage.at[piece], hbm.at[piece, columns, :], sems.at[n])
        for n, piece in enumerate(pieces(stage.shape[0]))
    ]
    for copy in copies:
        copy.start()
    return copies


def source_kernel(places, at_ref, rate_hbm, sid_hbm, key_hbm, value_hbm, soft_key_hbm, soft_value_hbm, soft_query_hbm, *rest):
    outs, rest = rest[:places], rest[places:]
    keys_by_head, values_by_head, pair_ref, give_ref, rate_ref, sid_ref, key_in, value_in, soft_key_in, soft_value_in, stage, sems = rest
    heads, tokens, width = keys_by_head.shape
    per, half = heads // places, heads // LOOK
    kv_heads = soft_key_in.shape[1]
    kv_half = kv_heads // LOOK
    span = 2 * kv_half * tokens
    rows = span + TAIL
    core, place = at_ref[0], at_ref[1]
    mine = pl.multiple_of(core * span, TAIL)
    theirs = pl.ds(pl.multiple_of((LOOK - 1 - core) * half, half), half)
    moves = (
        (soft_key_hbm, soft_key_in),
        (soft_value_hbm, soft_value_in),
        (sid_hbm, sid_ref),
        (rate_hbm, rate_ref),
        *[(hbm.at[piece], ref.at[piece]) for piece in pieces(tokens) for hbm, ref in ((key_hbm, key_in), (value_hbm, value_in))],
        (soft_query_hbm.at[:, theirs, :], give_ref.at[pl.ds(rows // half, tokens)]),
    )
    copies = [pltpu.make_async_copy(src, dst, sems.at[n]) for n, (src, dst) in enumerate(moves)]
    for copy in copies:
        copy.start()
    for at, ref in enumerate((soft_key_in, soft_value_in)):
        copies[at].wait()
        stage[...] = jnp.swapaxes(ref[...], 0, 1)
        for j in range(kv_half):
            start = (at * kv_half + j) * tokens
            pair_ref[pl.ds(mine + start, tokens), :] = stage[core * kv_half + j]
            block = stage[(LOOK - 1 - core) * kv_half + j]
            give_ref[pl.ds(start // half, tokens // half)] = block.reshape(tokens // half, half, width)
    copies[2].wait()
    sid_row = (sid_ref[...] + 1).astype(F32)
    tail = jnp.broadcast_to(sid_row, (TAIL, tokens)).astype(BF16)
    pair_ref[pl.ds(LOOK * span, TAIL), :] = tail
    give_ref[pl.ds(2 * kv_half * tokens // half, TAIL // half)] = tail.reshape(TAIL // half, half, tokens)
    open_row = (sid_row == jnp.max(sid_row, axis=1, keepdims=True)).astype(F32)
    behind = (tokens - 1 - lax.broadcasted_iota(jnp.int32, (1, tokens), 1)).astype(F32)
    copies[3].wait()
    for n, piece in enumerate(pieces(tokens)):
        copies[4 + 2 * n].wait()
        keys_by_head[:, piece, :] = jnp.swapaxes(key_in[piece], 0, 1)
        copies[5 + 2 * n].wait()
        values_by_head[:, piece, :] = jnp.swapaxes(value_in[piece], 0, 1)
    for k in range(places):
        for j in range(per):
            head = share_of(places, place ^ k) * per + j
            values = values_by_head[head]
            weighted = jnp.transpose(keys_by_head[head].astype(F32)) * (open_row * jnp.exp(-rate_ref[head] * behind))
            state = dot(weighted.astype(BF16), values, ((1,), (0,)))
            outs[k][pl.ds(j * width, width), :] = state.astype(BF16)
        outs[k][pl.ds(per * width, TAIL), :] = tail
        outs[k][pl.ds(per * width + TAIL, TAIL), :] = tail
    copies[-1].wait()


def pair_kernel(at_ref, got_ref, _, pair_ref):
    heads = got_ref.shape[1]
    width = pair_ref.shape[1]
    span = (pair_ref.shape[0] - TAIL) // LOOK
    other = 1 - at_ref[0]
    pair_ref[pl.ds(pl.multiple_of(other * span, TAIL), span), :] = got_ref[pl.ds(0, span // heads)].reshape(span, width)
    theirs = got_ref[pl.ds(span // heads, TAIL // heads)].reshape(TAIL, width)
    row_at = lax.broadcasted_iota(jnp.int32, (TAIL, width), 0)
    mine = pair_ref[pl.ds(LOOK * span, TAIL), :].astype(F32)
    tail = jnp.where(row_at // (TAIL // LOOK) == other, theirs.astype(F32), mine)
    pair_ref[pl.ds(LOOK * span, TAIL), :] = tail.astype(BF16)


def mix_kernel(places, at_ref, pair_ref, before_ref, *rest):
    home_ref, outs = rest[-places], rest[1 - places :]
    width = pair_ref.shape[1]
    span = (pair_ref.shape[0] - TAIL) // LOOK
    place = at_ref[1]
    for back, ref in enumerate((pair_ref, before_ref)):
        tails = ref[pl.ds(LOOK * span, TAIL), :].astype(F32)
        for block in range(LOOK):
            slot = LOOK * block + back
            home_ref[slot, pl.ds(0, span), :] = ref[pl.ds(block * span, span), :]
            row = block * (TAIL // LOOK)
            home_ref[slot, pl.ds(span, TAIL), :] = jnp.broadcast_to(tails[row : row + 1], (TAIL, width)).astype(BF16)
    for k in range(1, places):
        out = outs[k - 1]
        later = ((place ^ k) > place).astype(jnp.int32)
        out[0] = home_ref[0]
        out[1] = home_ref[3]
        out[2] = home_ref[1 + later]


def gather_slots(places, at_ref, pays, slots):
    for k in range(places):
        slots[at_ref[1] ^ k] = pays[k][pl.ds(0, slots.shape[1]), :]


def last_of(pay, per, width):
    return jnp.max(pay[pl.ds(per * width, TAIL), :].astype(F32), axis=(0, 1), keepdims=True)


def advance(pay, per, width, span, rates, state, last):
    now = last_of(pay, per, width)
    same = (now == last).astype(F32)
    state = [
        pay[pl.ds(j * width, width), :].astype(F32) + (same * jnp.exp(jnp.full((1, width), -rates[j] * span, F32))) * state[j]
        for j in range(per)
    ]
    return state, now


def store_state(ref, state, last):
    width = ref.shape[1]
    for j, value in enumerate(state):
        ref[pl.ds(j * width, width), :] = value.astype(BF16)
    tail = ref.shape[0] - len(state) * width
    ref[pl.ds(len(state) * width, tail), :] = jnp.broadcast_to(last, (tail, width)).astype(BF16)


def ending_kernel(places, tokens, at_ref, rate_ref, *rest):
    pays, outs, slots = rest[:places], rest[places : places + LOOK], rest[places + LOOK]
    width = outs[0].shape[1]
    per = (outs[0].shape[0] - TAIL) // width
    gather_slots(places, at_ref, pays, slots)
    rates = [rate_ref[share_of(places, at_ref[1]) * per + j] for j in range(per)]
    state = [jnp.zeros((width, width), F32)] * per
    last = jnp.zeros((1, 1), F32)
    for block in range(places):
        state, last = advance(slots.at[block], per, width, tokens, rates, state, last)
    for out_ref in outs:
        store_state(out_ref, state, last)


def prefix_kernel(places, tokens, at_ref, rate_ref, *rest):
    ahead, pays, outs = rest[:LOOK], rest[LOOK : LOOK + places], rest[LOOK + places : LOOK + 2 * places]
    slots, results = rest[LOOK + 2 * places :]
    width = ahead[0].shape[1]
    per = (ahead[0].shape[0] - TAIL) // width
    gather_slots(places, at_ref, pays, slots)
    rates = [rate_ref[share_of(places, at_ref[1]) * per + j] for j in range(per)]
    state = [ahead[-1][pl.ds(j * width, width), :].astype(F32) for j in range(per)]
    last = last_of(ahead[-1], per, width)
    for group in reversed(ahead[:-1]):
        state, last = advance(group, per, width, places * tokens, rates, state, last)
    for block in range(places):
        store_state(results.at[block], state, last)
        if block < places - 1:
            state, last = advance(slots.at[block], per, width, tokens, rates, state, last)
    for k in range(places):
        outs[k][...] = results[at_ref[1] ^ k]


def prep_kernel(rate_ref, sid_ref, query_ref, keys_by_head, left_ref):
    heads, tokens, _ = keys_by_head.shape
    sid_row = (sid_ref[...] + 1).astype(F32)
    row_at = lax.broadcasted_iota(jnp.int32, (tokens, tokens), 0)
    lane = lax.broadcasted_iota(jnp.int32, (tokens, tokens), 1)
    allowed = ((row_at >= lane) & (column(sid_row) == sid_row)).astype(F32)
    ahead = (lax.broadcasted_iota(jnp.int32, (1, tokens), 1) + 1).astype(F32)
    left_ref[:, :, tokens:] = jnp.swapaxes(query_ref[...], 0, 1)
    for head in range(heads):
        weights = dot(left_ref[head, :, tokens:], keys_by_head[head], ((1,), (1,)))
        weights = weights * allowed * jnp.exp(rate_ref[head] * ahead)
        left_ref[head, :, :tokens] = weights.astype(BF16)


class Light:
    def __init__(self, places, at_ref, rate_ref, sid_ref, gain_ref, left_ref, values_by_head, pay):
        self.rate_ref, self.gain_ref, self.left_ref, self.values_by_head = rate_ref, gain_ref, left_ref, values_by_head
        heads, self.tokens, self.width = values_by_head.shape
        self.places, self.place, self.core = places, at_ref[1], at_ref[0]
        self.half, self.per = heads // LOOK, heads // places
        sid_column = column((sid_ref[...] + 1).astype(F32))
        self.continues = (sid_column == last_of(pay, self.per, self.width)).astype(BF16)
        self.ahead = (lax.broadcasted_iota(jnp.int32, (self.tokens, 1), 0) + 1).astype(F32)

    def columns(self, which):
        return pl.ds(pl.multiple_of(which * self.half, self.half), self.half)

    def half_out(self, ks, pays, light_hbm, by_head, stage, sems):
        which = odd(self.place ^ ks[0])
        for k, pay in zip(ks, pays):
            for j in range(self.per):
                head = share_of(self.places, self.place ^ k) * self.per + j
                tokens = self.tokens
                left = jnp.concatenate([self.left_ref[head, :, :tokens], self.left_ref[head, :, tokens:] * self.continues], 1)
                right = jnp.concatenate([self.values_by_head[head], pay[pl.ds(j * self.width, self.width), :]], 0)
                raw = dot(left, right, ((1,), (0,)))
                lead = jnp.exp(-self.rate_ref[head] * self.ahead)
                mean_square = jnp.mean(raw * raw, axis=1, keepdims=True) * (lead * lead)
                out = raw * (lead * lax.rsqrt(mean_square + NORM_EPS)) * self.gain_ref[pl.ds(head, 1), :]
                by_head[head - which * self.half] = out.astype(BF16)
        stage[...] = jnp.swapaxes(by_head[...], 0, 1)
        for copy in copy_out(stage, light_hbm, self.columns(which), sems):
            copy.wait()


def first_kernel(places, ks, at_ref, rate_ref, sid_ref, gain_ref, left_ref, values_by_head, keep_ref, *rest):
    pays, rest = rest[PARTS : PARTS + len(ks)], rest[PARTS + len(ks) :]
    light_hbm, soft_hbm, (by_head, stage, sems) = rest[0], rest[1], rest[2 + PARTS :]
    light = Light(places, at_ref, rate_ref, sid_ref, gain_ref, left_ref, values_by_head, pays[0])
    copy = pltpu.make_async_copy(keep_ref, soft_hbm.at[:, light.columns(light.core), :], sems.at[0])
    copy.start()
    light.half_out(ks, pays, light_hbm, by_head, stage, sems.at[pl.ds(1, PIECES)])
    copy.wait()


def second_kernel(places, ks, at_ref, rate_ref, sid_ref, gain_ref, left_ref, values_by_head, *rest):
    got, rest = rest[:PARTS], rest[PARTS + 2 :]
    pays, (light_hbm, soft_hbm, by_head, stage, sems) = rest[: len(ks)], rest[len(ks) :]
    light = Light(places, at_ref, rate_ref, sid_ref, gain_ref, left_ref, values_by_head, pays[0])
    size = light.tokens // PARTS
    copies = []
    for n in range(PARTS):
        there = soft_hbm.at[pl.ds(n * size, size), light.columns(LOOK - 1 - light.core), :]
        copies.append(pltpu.make_async_copy(got[n], there, sems.at[PIECES + n]))
        copies[-1].start()
    light.half_out(ks, pays, light_hbm, by_head, stage, sems)
    for copy in copies:
        copy.wait()


class Soft:
    def __init__(self, places, at_ref, query_ref, got_ref, home_ref, share, codes):
        self.core, self.place = at_ref[0], at_ref[1]
        self.tokens, _, self.width = query_ref.shape
        self.share, self.heads, self.rows = share, got_ref.shape[1], home_ref.shape[1]
        self.kv_heads = self.heads // share
        self.query_ref, self.got_ref, self.codes = query_ref, got_ref, codes
        self.lane = lax.broadcasted_iota(jnp.int32, (self.tokens, self.tokens), 1)
        self.factor = self.width ** (-0.5) * math.log2(math.e)

    def spread(self, value):
        tokens, share = self.tokens, self.share
        value = jnp.broadcast_to(value.reshape(tokens, 1, tokens), (tokens, share, tokens))
        return value.reshape(tokens * share, tokens)

    def marked(self, pick):
        ref, slot = pick
        sids = ref[slot, pl.ds(2 * self.kv_heads * self.tokens, TAIL), :].astype(F32)[0:1, :]
        return column(sids) == self.lane.astype(F32)

    def far(self, block, ks, pays):
        picks = []
        for k, pay in zip(ks, pays):
            later = ((self.place ^ k) > self.place).astype(jnp.int32)
            picks.append((pay, 2 * later * (1 - block)))
            picks.append((pay, 1 + (1 - later) * block))
        return picks

    def code(self, own, picks):
        for at, pick in enumerate(picks):
            self.codes[own, pl.ds(at * self.tokens, self.tokens), :] = self.marked(pick).astype(BF16)

    def query(self, own, g):
        tokens, share = self.tokens, self.share
        if own:
            first = pl.multiple_of(self.core * self.heads, self.heads)
            wide = self.query_ref[:, pl.ds(first, self.heads), :]
        else:
            wide = self.got_ref[pl.ds(self.rows // self.heads, tokens)]
        wide = wide.astype(F32)[:, g * share : (g + 1) * share, :]
        return wide.reshape(tokens * share, self.width).astype(BF16)

    def scores(self, own, g, marks, picks):
        tokens = self.tokens
        query = jnp.concatenate([self.query(own, g), marks], 1)
        keys = jnp.concatenate([ref[slot, pl.ds(g * tokens, tokens), :] for ref, slot in picks], 0)
        codes = self.codes[own, pl.ds(0, len(picks) * tokens), :]
        return dot(query, jnp.concatenate([keys, codes], 1), ((1,), (1,)))

    def probs(self, scores, peak):
        wide = jnp.concatenate([peak] * (scores.shape[1] // self.width), 1)
        return jnp.exp2((scores - wide) * self.factor).astype(BF16)

    def mixed(self, g, probs, picks):
        tokens = self.tokens
        rows = pl.ds((self.kv_heads + g) * tokens, tokens)
        values = jnp.concatenate([ref[slot, rows, :] for ref, slot in picks], 0)
        return dot(probs, jnp.concatenate([values, jnp.ones_like(values)], 1), ((1,), (0,)))

    def top(self, scores):
        return jnp.broadcast_to(jnp.max(scores, axis=1, keepdims=True), (scores.shape[0], self.width))

    def added(self, own, g, marks, picks, sums, before):
        scores = self.scores(own, g, marks, picks)
        peak = jnp.maximum(before, self.top(scores))
        scale = jnp.exp2((before - peak) * self.factor)
        out = self.mixed(g, self.probs(scores, peak), picks) + sums * jnp.concatenate([scale, scale], 1)
        return out, peak


def home_kernel(places, share, at_ref, got_ref, query_ref, home_ref, sums_ref, peaks_ref, marks_ref, codes, fills):
    soft = Soft(places, at_ref, query_ref, got_ref, home_ref, share, codes)
    row_at = lax.broadcasted_iota(jnp.int32, soft.lane.shape, 0)
    fills[...] = soft.spread(jnp.where(row_at >= soft.lane, 0.0, NEG_FILL))
    for own in range(LOOK):
        block = soft.core if own else 1 - soft.core
        mine = (home_ref, 2 * block)
        picks = [(home_ref, 1 - block), (home_ref, 3), mine]
        soft.code(own, picks)
        marks_ref[own] = soft.spread(jnp.where(soft.marked(mine), 0.0, NEG_FILL)).astype(BF16)
        last = (len(picks) - 1) * soft.tokens
        for g in range(soft.kv_heads):
            scores = soft.scores(own, g, marks_ref[own], picks)
            scores = jnp.concatenate([scores[:, :last], scores[:, last:] + fills[...]], 1)
            peak = soft.top(scores)
            at = own * soft.kv_heads + g
            sums_ref[at] = soft.mixed(g, soft.probs(scores, peak), picks)
            peaks_ref[at] = peak


def away_kernel(places, share, at_ref, got_ref, query_ref, home_ref, sums_ref, peaks_ref, marks_ref, *rest):
    pays, rest = rest[: places - 1], rest[places - 1 :]
    given, kept, codes = rest[:PARTS], rest[PARTS], rest[PARTS + 1]
    soft = Soft(places, at_ref, query_ref, got_ref, home_ref, share, codes)
    for own in range(LOOK):
        picks = soft.far(soft.core if own else 1 - soft.core, range(1, places), pays)
        soft.code(own, picks)
        mixed = []
        for g in range(soft.kv_heads):
            at = own * soft.kv_heads + g
            out, _ = soft.added(own, g, marks_ref[own], picks, sums_ref[at], peaks_ref[at])
            mixed.append((out[:, : soft.width] / out[:, soft.width :]).reshape(soft.tokens, share, soft.width))
        mixed = jnp.concatenate(mixed, 1).astype(BF16)
        if own:
            kept[...] = mixed
        else:
            size = soft.tokens // PARTS
            for n in range(PARTS):
                given[n][...] = mixed[n * size : (n + 1) * size]


def body(
    light_query,
    light_keys,
    light_values,
    decay_rate,
    norm_gain,
    soft_query,
    soft_keys,
    soft_values,
    segment_ids,
):
    places = lax.axis_size("head")
    n_all = lax.axis_size("ctx") * places
    members = LOOK * places
    core = lax.rem(lax.axis_index("ctx"), LOOK)
    place = lax.axis_index("head")
    at = jnp.stack([core, place, core * places + place]).astype(jnp.int32)
    tokens, heads, width = light_query.shape
    kv_heads = soft_keys.shape[1]
    per, half, kv_half = heads // places, heads // LOOK, kv_heads // LOOK
    sid_row = segment_ids.reshape(1, tokens)
    even, uneven = [k for k in range(places) if not odd(k)], [k for k in range(places) if odd(k)]

    def partner(value, k):
        pairs = [(i, i - i % members + ((i % members) ^ k)) for i in range(n_all)]
        return lax.ppermute(value, AXES, pairs)

    def across(value):
        return partner(value, places)

    def to_places(values):
        return [values[0]] + [partner(values[k], k) for k in range(1, places)]

    def onward(value, groups):
        step = groups * places
        return lax.ppermute(value, AXES, [(i, i + step) for i in range(n_all - step)])

    def shape(*dims):
        return jax.ShapeDtypeStruct(dims, BF16)

    def room(*dims, dtype=BF16):
        return pltpu.VMEM(dims, dtype)

    def semaphores(count):
        return pltpu.SemaphoreType.DMA((count,))

    pay = shape(2 * kv_half * tokens + TAIL, width)
    pair = shape(LOOK * (pay.shape[0] - TAIL) + TAIL, width)
    given = shape(pay.shape[0] // half + tokens, half, width)
    state = shape(per * width + TAIL, width)
    by_head = shape(heads, tokens, width)
    half_out = shape(tokens, half, width)
    slots = room(places, *state.shape)
    sid_room = room(1, tokens, dtype=jnp.int32)

    def held(value):
        return pltpu.with_memory_space_constraint(value, pltpu.HBM)

    made = call(
        functools.partial(source_kernel, places), "source", 0, 16, [SMEM] + [HBM] * 7,
        [shape(state.shape[0] + TAIL, width)] * places + [by_head] * 2 + [pair, given], [VMEM] * (places + 4),
        [pltpu.SMEM((heads,), F32), sid_room] + [room(tokens, heads, width)] * 2 + [room(tokens, kv_heads, width)] * 2
        + [room(kv_heads, tokens, width), semaphores(5 + 2 * PIECES)],
    )(at, *[held(x) for x in (decay_rate, sid_row, light_keys, light_values, soft_keys, soft_values, soft_query)])
    keys_by_head, values_by_head, own, give = made[places:]
    states = to_places(made[:places])
    got = across(give)
    own = call(pair_kernel, "pair", 0, 8, [SMEM, VMEM, VMEM], pair, VMEM, aliases={2: 0})(at, got, own)
    before = onward(own, LOOK)

    left = call(
        prep_kernel, "prep", 0, 16, [SMEM, VMEM, VMEM, VMEM], shape(heads, tokens, tokens + width), VMEM
    )(decay_rate, sid_row, light_query, keys_by_head)
    mixed = call(
        functools.partial(mix_kernel, places), "mix", 0, 8, [SMEM] + [VMEM] * 2,
        [shape(4, *pay.shape)] + [shape(3, *pay.shape)] * (places - 1), [VMEM] * places, after=[left, *[states[k] for k in even[1:]]],
    )(at, own, before)
    home = mixed[0]
    parcels = to_places(mixed)

    ending = call(
        functools.partial(ending_kernel, places, tokens), "ending", 0, 8, [SMEM] * 2 + [VMEM] * places,
        [state] * LOOK, [VMEM] * LOOK, [slots], after=[home],
    )(at, decay_rate, *states)
    ahead = [onward(ending[n], n + 1) for n in range(LOOK)]
    share = half // kv_half
    queries = tokens * share

    def codes(blocks):
        return room(LOOK, blocks * tokens, width)

    def limit(blocks):
        return (blocks * tokens * queries * 14 + 8 * half_out.size) / 2**20 + 8

    sums_like = [
        jax.ShapeDtypeStruct((LOOK * kv_half, queries, 2 * width), F32),
        jax.ShapeDtypeStruct((LOOK * kv_half, queries, width), F32),
    ]
    sums, peaks, marks = call(
        functools.partial(home_kernel, places, share), "home", 0, limit(3), [SMEM] + [VMEM] * 3,
        sums_like + [shape(LOOK, queries, tokens)], [VMEM] * 3, [codes(3), room(queries, tokens, dtype=F32)], after=[ending[0]],
    )(at, got, soft_query, home)
    prefixed = call(
        functools.partial(prefix_kernel, places, tokens), "prefix", 0, 12, [SMEM] * 2 + [VMEM] * (places + LOOK),
        [state] * places, [VMEM] * places, [slots, slots], after=[sums],
    )(at, decay_rate, *ahead, *states)
    entries = to_places(prefixed)

    blocks = 2 * (places - 1)
    part_out = shape(tokens // PARTS, half, width)
    made = call(
        functools.partial(away_kernel, places, share), "away", 30, limit(blocks), [SMEM] + [VMEM] * (5 + places),
        [part_out] * PARTS + [half_out], [VMEM] * (PARTS + 1), [codes(blocks)], after=[prefixed[0]],
    )(at, got, soft_query, home, sums, peaks, marks, *parcels[1:])
    soft_theirs, soft_kept = made[:PARTS], made[PARTS]

    whole = shape(tokens, heads, width)
    known = (at, decay_rate, sid_row, norm_gain, left, values_by_head)
    rooms = [room(half, tokens, width), room(tokens, half, width)]
    made = call(
        functools.partial(first_kernel, places, even), "first", 0, 16,
        [SMEM] * 2 + [VMEM] * 5 + [ANY] * PARTS + [VMEM] * len(even), [whole, whole] + [part_out] * PARTS, [HBM, HBM] + [ANY] * PARTS,
        rooms + [semaphores(1 + PIECES)], aliases={7 + n: 2 + n for n in range(PARTS)},
    )(*known, soft_kept, *soft_theirs, *[entries[k] for k in even])
    soft_got = [across(x) for x in made[2:]]
    return tuple(
        call(
            functools.partial(second_kernel, places, uneven), "second", 15, 16,
            [SMEM] * 2 + [VMEM] * (4 + PARTS) + [HBM] * 2 + [VMEM] * len(uneven), [whole, whole], [HBM, HBM],
            rooms + [semaphores(PIECES + PARTS)], aliases={6 + PARTS: 0, 7 + PARTS: 1},
        )(*known, *soft_got, made[0], made[1], *[entries[k] for k in uneven])
    )


def solution(mesh):
    placed = P(("ctx", "head"), None, None)
    return jax.shard_map(
        body,
        mesh=mesh,
        in_specs=(placed, placed, placed, P(), P(), placed, placed, placed, P(("ctx", "head"))),
        out_specs=(placed, placed),
        check_vma=False,
    )
```

```python
import functools
import math

import jax
import jax.numpy as jnp
from jax import lax
from jax.experimental import pallas as pl
from jax.experimental.pallas import tpu as pltpu
from jax.sharding import PartitionSpec as P

LOOK = 2
PARTS = 2
PIECES = 4
NEG_FILL = -1e30
NORM_EPS = 1e-06
TAIL = 16
F32 = jnp.float32
BF16 = jnp.bfloat16
AXES = ("ctx", "head")
VMEM = pl.BlockSpec(memory_space=pltpu.VMEM)
SMEM = pl.BlockSpec(memory_space=pltpu.SMEM)
ANY = pl.BlockSpec(memory_space=pl.ANY)
HBM = pl.BlockSpec(memory_space=pltpu.HBM)


def call(kernel, name, micros, limit_mib, ins, outs, out_specs, scratch=(), aliases=None, after=()):
    count = len(ins)

    def run(*refs):
        kernel(*refs[:count], *refs[count + len(after) :])

    made = pl.pallas_call(
        run,
        out_shape=outs,
        in_specs=list(ins) + [ANY] * len(after),
        out_specs=out_specs,
        scratch_shapes=list(scratch),
        input_output_aliases=aliases or {},
        compiler_params=pltpu.CompilerParams(vmem_limit_bytes=int(limit_mib * 1024 * 1024)),
        cost_estimate=pl.CostEstimate(flops=int(micros * 1e9), bytes_accessed=0, transcendentals=0),
        name=name,
    )
    return lambda *args: made(*args, *after)


def column(row):
    size = row.shape[1]
    return jnp.transpose(jnp.broadcast_to(row, (size, size)))


def dot(left, right, contract):
    return lax.dot_general(left, right, (contract, ((), ())), preferred_element_type=F32)


def odd(place):
    for shift in (8, 4, 2, 1):
        place = place ^ (place >> shift)
    return place & 1


def share_of(places, place):
    return odd(place) * (places // 2) + (place >> 1)


def pieces(tokens):
    return [pl.ds(n * (tokens // PIECES), tokens // PIECES) for n in range(PIECES)]


def copy_out(stage, hbm, columns, sems):
    copies = [
        pltpu.make_async_copy(stage.at[piece], hbm.at[piece, columns, :], sems.at[n])
        for n, piece in enumerate(pieces(stage.shape[0]))
    ]
    for copy in copies:
        copy.start()
    return copies


def split(value):
    high = value.astype(BF16)
    return high, (value - high.astype(F32)).astype(BF16)


def source_kernel(places, at_ref, rate_hbm, sid_hbm, key_hbm, value_hbm, soft_key_hbm, soft_value_hbm, soft_query_hbm, *rest):
    outs, rest = rest[:places], rest[places:]
    keys_by_head, values_by_head, pair_ref, give_ref, rate_ref, sid_ref, key_in, value_in, soft_key_in, soft_value_in, stage, sems = rest
    heads, tokens, width = keys_by_head.shape
    per, half = heads // places, heads // LOOK
    kv_heads = soft_key_in.shape[1]
    kv_half = kv_heads // LOOK
    span = 2 * kv_half * tokens
    rows = span + TAIL
    core, place = at_ref[0], at_ref[1]
    mine = pl.multiple_of(core * span, TAIL)
    theirs = pl.ds(pl.multiple_of((LOOK - 1 - core) * half, half), half)
    moves = (
        (soft_key_hbm, soft_key_in),
        (soft_value_hbm, soft_value_in),
        (sid_hbm, sid_ref),
        (rate_hbm, rate_ref),
        *[(hbm.at[piece], ref.at[piece]) for piece in pieces(tokens) for hbm, ref in ((key_hbm, key_in), (value_hbm, value_in))],
        (soft_query_hbm.at[:, theirs, :], give_ref.at[pl.ds(rows // half, tokens)]),
    )
    copies = [pltpu.make_async_copy(src, dst, sems.at[n]) for n, (src, dst) in enumerate(moves)]
    for copy in copies:
        copy.start()
    for at, ref in enumerate((soft_key_in, soft_value_in)):
        copies[at].wait()
        stage[...] = jnp.swapaxes(ref[...], 0, 1)
        for j in range(kv_half):
            start = (at * kv_half + j) * tokens
            pair_ref[pl.ds(mine + start, tokens), :] = stage[core * kv_half + j]
            block = stage[(LOOK - 1 - core) * kv_half + j]
            give_ref[pl.ds(start // half, tokens // half)] = block.reshape(tokens // half, half, width)
    copies[2].wait()
    sid_row = (sid_ref[...] + 1).astype(F32)
    tail = jnp.broadcast_to(sid_row, (TAIL, tokens)).astype(BF16)
    pair_ref[pl.ds(LOOK * span, TAIL), :] = tail
    give_ref[pl.ds(2 * kv_half * tokens // half, TAIL // half)] = tail.reshape(TAIL // half, half, tokens)
    open_row = (sid_row == jnp.max(sid_row, axis=1, keepdims=True)).astype(F32)
    behind = (tokens - 1 - lax.broadcasted_iota(jnp.int32, (1, tokens), 1)).astype(F32)
    copies[3].wait()
    for n, piece in enumerate(pieces(tokens)):
        copies[4 + 2 * n].wait()
        keys_by_head[:, piece, :] = jnp.swapaxes(key_in[piece], 0, 1)
        copies[5 + 2 * n].wait()
        values_by_head[:, piece, :] = jnp.swapaxes(value_in[piece], 0, 1)
    for k in range(places):
        for j in range(per):
            head = share_of(places, place ^ k) * per + j
            values = values_by_head[head]
            weighted = jnp.transpose(keys_by_head[head].astype(F32)) * (open_row * jnp.exp(-rate_ref[head] * behind))
            high, low = split(weighted)
            state = dot(jnp.concatenate([high, low], 1), jnp.concatenate([values, values], 0), ((1,), (0,)))
            outs[k][pl.ds(j * width, width), :] = state.astype(BF16)
        outs[k][pl.ds(per * width, TAIL), :] = tail
        outs[k][pl.ds(per * width + TAIL, TAIL), :] = tail
    copies[-1].wait()


def pair_kernel(at_ref, got_ref, _, pair_ref):
    heads = got_ref.shape[1]
    width = pair_ref.shape[1]
    span = (pair_ref.shape[0] - TAIL) // LOOK
    other = 1 - at_ref[0]
    pair_ref[pl.ds(pl.multiple_of(other * span, TAIL), span), :] = got_ref[pl.ds(0, span // heads)].reshape(span, width)
    theirs = got_ref[pl.ds(span // heads, TAIL // heads)].reshape(TAIL, width)
    row_at = lax.broadcasted_iota(jnp.int32, (TAIL, width), 0)
    mine = pair_ref[pl.ds(LOOK * span, TAIL), :].astype(F32)
    tail = jnp.where(row_at // (TAIL // LOOK) == other, theirs.astype(F32), mine)
    pair_ref[pl.ds(LOOK * span, TAIL), :] = tail.astype(BF16)


def mix_kernel(places, at_ref, pair_ref, before_ref, *rest):
    home_ref, outs = rest[-places], rest[1 - places :]
    width = pair_ref.shape[1]
    span = (pair_ref.shape[0] - TAIL) // LOOK
    place = at_ref[1]
    for back, ref in enumerate((pair_ref, before_ref)):
        tails = ref[pl.ds(LOOK * span, TAIL), :].astype(F32)
        for block in range(LOOK):
            slot = LOOK * block + back
            home_ref[slot, pl.ds(0, span), :] = ref[pl.ds(block * span, span), :]
            row = block * (TAIL // LOOK)
            home_ref[slot, pl.ds(span, TAIL), :] = jnp.broadcast_to(tails[row : row + 1], (TAIL, width)).astype(BF16)
    row_at = lax.broadcasted_iota(jnp.int32, (TAIL, width), 0)
    for k in range(1, places):
        out = outs[k - 1]
        later = ((place ^ k) > place).astype(jnp.int32)
        tail = jnp.zeros((TAIL, width), F32)
        for n, slot in enumerate((0, 3, 1 + later)):
            out[pl.ds(n * span, span), :] = home_ref[slot, pl.ds(0, span), :]
            tail = jnp.where(row_at == n, home_ref[slot, pl.ds(span, TAIL), :].astype(F32), tail)
        out[pl.ds(3 * span, TAIL), :] = tail.astype(BF16)


def gather_slots(places, at_ref, pays, slots):
    for k in range(places):
        slots[at_ref[1] ^ k] = pays[k][pl.ds(0, slots.shape[1]), :]


def last_of(pay, per, width):
    return jnp.max(pay[pl.ds(per * width, TAIL), :].astype(F32), axis=(0, 1), keepdims=True)


def advance(pay, per, width, span, rates, state, last):
    now = last_of(pay, per, width)
    same = (now == last).astype(F32)
    state = [
        pay[pl.ds(j * width, width), :].astype(F32) + (same * jnp.exp(jnp.full((1, width), -rates[j] * span, F32))) * state[j]
        for j in range(per)
    ]
    return state, now


def store_state(ref, state, last):
    width = ref.shape[1]
    for j, value in enumerate(state):
        ref[pl.ds(j * width, width), :] = value.astype(BF16)
    tail = ref.shape[0] - len(state) * width
    ref[pl.ds(len(state) * width, tail), :] = jnp.broadcast_to(last, (tail, width)).astype(BF16)


def ending_kernel(places, tokens, at_ref, rate_ref, *rest):
    pays, outs, slots = rest[:places], rest[places : places + LOOK], rest[places + LOOK]
    width = outs[0].shape[1]
    per = (outs[0].shape[0] - TAIL) // width
    gather_slots(places, at_ref, pays, slots)
    rates = [rate_ref[share_of(places, at_ref[1]) * per + j] for j in range(per)]
    state = [jnp.zeros((width, width), F32)] * per
    last = jnp.zeros((1, 1), F32)
    for block in range(places):
        state, last = advance(slots.at[block], per, width, tokens, rates, state, last)
    for out_ref in outs:
        store_state(out_ref, state, last)


def prefix_kernel(places, tokens, at_ref, rate_ref, *rest):
    ahead, pays, outs = rest[:LOOK], rest[LOOK : LOOK + places], rest[LOOK + places : LOOK + 2 * places]
    slots, results = rest[LOOK + 2 * places :]
    width = ahead[0].shape[1]
    per = (ahead[0].shape[0] - TAIL) // width
    gather_slots(places, at_ref, pays, slots)
    rates = [rate_ref[share_of(places, at_ref[1]) * per + j] for j in range(per)]
    state = [ahead[-1][pl.ds(j * width, width), :].astype(F32) for j in range(per)]
    last = last_of(ahead[-1], per, width)
    for group in reversed(ahead[:-1]):
        state, last = advance(group, per, width, places * tokens, rates, state, last)
    for block in range(places):
        store_state(results.at[block], state, last)
        if block < places - 1:
            state, last = advance(slots.at[block], per, width, tokens, rates, state, last)
    for k in range(places):
        outs[k][...] = results[at_ref[1] ^ k]


def prep_kernel(rate_ref, sid_ref, query_ref, keys_by_head, left_ref):
    heads, tokens, _ = keys_by_head.shape
    sid_row = (sid_ref[...] + 1).astype(F32)
    row_at = lax.broadcasted_iota(jnp.int32, (tokens, tokens), 0)
    lane = lax.broadcasted_iota(jnp.int32, (tokens, tokens), 1)
    allowed = ((row_at >= lane) & (column(sid_row) == sid_row)).astype(F32)
    ahead = (lax.broadcasted_iota(jnp.int32, (1, tokens), 1) + 1).astype(F32)
    left_ref[:, :, tokens:] = jnp.swapaxes(query_ref[...], 0, 1)
    for head in range(heads):
        weights = dot(left_ref[head, :, tokens:], keys_by_head[head], ((1,), (1,)))
        weights = weights * allowed * jnp.exp(rate_ref[head] * ahead)
        left_ref[head, :, :tokens] = weights.astype(BF16)


class Light:
    def __init__(self, places, at_ref, rate_ref, sid_ref, gain_ref, left_ref, values_by_head, pay):
        self.rate_ref, self.gain_ref, self.left_ref, self.values_by_head = rate_ref, gain_ref, left_ref, values_by_head
        heads, self.tokens, self.width = values_by_head.shape
        self.places, self.place, self.core = places, at_ref[1], at_ref[0]
        self.half, self.per = heads // LOOK, heads // places
        sid_column = column((sid_ref[...] + 1).astype(F32))
        self.continues = (sid_column == last_of(pay, self.per, self.width)).astype(BF16)
        self.ahead = (lax.broadcasted_iota(jnp.int32, (self.tokens, 1), 0) + 1).astype(F32)

    def columns(self, which):
        return pl.ds(pl.multiple_of(which * self.half, self.half), self.half)

    def half_out(self, ks, pays, light_hbm, by_head, stage, sems):
        which = odd(self.place ^ ks[0])
        for k, pay in zip(ks, pays):
            for j in range(self.per):
                head = share_of(self.places, self.place ^ k) * self.per + j
                tokens = self.tokens
                left = jnp.concatenate([self.left_ref[head, :, :tokens], self.left_ref[head, :, tokens:] * self.continues], 1)
                right = jnp.concatenate([self.values_by_head[head], pay[pl.ds(j * self.width, self.width), :]], 0)
                raw = dot(left, right, ((1,), (0,)))
                lead = jnp.exp(-self.rate_ref[head] * self.ahead)
                mean_square = jnp.mean(raw * raw, axis=1, keepdims=True) * (lead * lead)
                out = raw * (lead * lax.rsqrt(mean_square + NORM_EPS)) * self.gain_ref[pl.ds(head, 1), :]
                by_head[head - which * self.half] = out.astype(BF16)
        stage[...] = jnp.swapaxes(by_head[...], 0, 1)
        for copy in copy_out(stage, light_hbm, self.columns(which), sems):
            copy.wait()


def first_kernel(places, ks, at_ref, rate_ref, sid_ref, gain_ref, left_ref, values_by_head, keep_ref, *rest):
    pays, rest = rest[PARTS : PARTS + len(ks)], rest[PARTS + len(ks) :]
    light_hbm, soft_hbm, (by_head, stage, sems) = rest[0], rest[1], rest[2 + PARTS :]
    light = Light(places, at_ref, rate_ref, sid_ref, gain_ref, left_ref, values_by_head, pays[0])
    copy = pltpu.make_async_copy(keep_ref, soft_hbm.at[:, light.columns(light.core), :], sems.at[0])
    copy.start()
    light.half_out(ks, pays, light_hbm, by_head, stage, sems.at[pl.ds(1, PIECES)])
    copy.wait()


def second_kernel(places, ks, at_ref, rate_ref, sid_ref, gain_ref, left_ref, values_by_head, *rest):
    got, rest = rest[:PARTS], rest[PARTS + 2 :]
    pays, (light_hbm, soft_hbm, by_head, stage, sems) = rest[: len(ks)], rest[len(ks) :]
    light = Light(places, at_ref, rate_ref, sid_ref, gain_ref, left_ref, values_by_head, pays[0])
    size = light.tokens // PARTS
    copies = []
    for n in range(PARTS):
        there = soft_hbm.at[pl.ds(n * size, size), light.columns(LOOK - 1 - light.core), :]
        copies.append(pltpu.make_async_copy(got[n], there, sems.at[PIECES + n]))
        copies[-1].start()
    light.half_out(ks, pays, light_hbm, by_head, stage, sems)
    for copy in copies:
        copy.wait()


class Soft:
    def __init__(self, places, at_ref, query_ref, got_ref, home_ref, share, codes):
        self.core, self.place = at_ref[0], at_ref[1]
        self.tokens, _, self.width = query_ref.shape
        self.share, self.heads, self.rows = share, got_ref.shape[1], home_ref.shape[1]
        self.kv_heads = self.heads // share
        self.query_ref, self.got_ref, self.codes = query_ref, got_ref, codes
        self.lane = lax.broadcasted_iota(jnp.int32, (self.tokens, self.tokens), 1)
        self.factor = self.width ** (-0.5) * math.log2(math.e)

    def spread(self, value):
        tokens, share = self.tokens, self.share
        value = jnp.broadcast_to(value.reshape(tokens, 1, tokens), (tokens, share, tokens))
        return value.reshape(tokens * share, tokens)

    def marked(self, pick):
        ref, slot = pick
        span = 2 * self.kv_heads * self.tokens
        if len(ref.shape) == 3:
            sids = ref[slot, pl.ds(span, TAIL), :].astype(F32)[0:1, :]
        else:
            tail = ref[pl.ds(ref.shape[0] - TAIL, TAIL), :].astype(F32)
            row_at = lax.broadcasted_iota(jnp.int32, tail.shape, 0)
            sids = jnp.sum(jnp.where(row_at == slot, tail, 0.0), axis=0, keepdims=True)
        return column(sids) == self.lane.astype(F32)

    def part(self, pick, n):
        ref, slot = pick
        if len(ref.shape) == 3:
            return ref[slot, pl.ds(n * self.tokens, self.tokens), :]
        start = slot * (2 * self.kv_heads * self.tokens) + n * self.tokens
        return ref[pl.ds(pl.multiple_of(start, TAIL), self.tokens), :]

    def far(self, block, ks, pays):
        picks = []
        for k, pay in zip(ks, pays):
            later = ((self.place ^ k) > self.place).astype(jnp.int32)
            picks.append((pay, 2 * later * (1 - block)))
            picks.append((pay, 1 + (1 - later) * block))
        return picks

    def code(self, own, picks):
        for at, pick in enumerate(picks):
            self.codes[own, pl.ds(at * self.tokens, self.tokens), :] = self.marked(pick).astype(BF16)

    def query(self, own, g):
        tokens, share = self.tokens, self.share
        if own:
            first = pl.multiple_of(self.core * self.heads, self.heads)
            wide = self.query_ref[:, pl.ds(first, self.heads), :]
        else:
            wide = self.got_ref[pl.ds(self.rows // self.heads, tokens)]
        wide = wide.astype(F32)[:, g * share : (g + 1) * share, :]
        return wide.reshape(tokens * share, self.width).astype(BF16)

    def scores(self, own, g, marks, picks):
        tokens = self.tokens
        query = jnp.concatenate([self.query(own, g), marks], 1)
        keys = jnp.concatenate([self.part(pick, g) for pick in picks], 0)
        codes = self.codes[own, pl.ds(0, len(picks) * tokens), :]
        return dot(query, jnp.concatenate([keys, codes], 1), ((1,), (1,)))

    def probs(self, scores, peak):
        wide = jnp.concatenate([peak] * (scores.shape[1] // self.width), 1)
        return jnp.exp2((scores - wide) * self.factor).astype(BF16)

    def mixed(self, g, probs, picks):
        values = jnp.concatenate([self.part(pick, self.kv_heads + g) for pick in picks], 0)
        return dot(probs, jnp.concatenate([values, jnp.ones_like(values)], 1), ((1,), (0,)))

    def top(self, scores):
        return jnp.broadcast_to(jnp.max(scores, axis=1, keepdims=True), (scores.shape[0], self.width))

    def added(self, own, g, marks, picks, sums, before):
        scores = self.scores(own, g, marks, picks)
        peak = jnp.maximum(before, self.top(scores))
        scale = jnp.exp2((before - peak) * self.factor)
        out = self.mixed(g, self.probs(scores, peak), picks) + sums * jnp.concatenate([scale, scale], 1)
        return out, peak


def home_kernel(places, share, at_ref, got_ref, query_ref, home_ref, sums_ref, peaks_ref, marks_ref, codes, fills):
    soft = Soft(places, at_ref, query_ref, got_ref, home_ref, share, codes)
    row_at = lax.broadcasted_iota(jnp.int32, soft.lane.shape, 0)
    fills[...] = soft.spread(jnp.where(row_at >= soft.lane, 0.0, NEG_FILL))
    for own in range(LOOK):
        block = soft.core if own else 1 - soft.core
        mine = (home_ref, 2 * block)
        picks = [(home_ref, 1 - block), (home_ref, 3), mine]
        soft.code(own, picks)
        marks_ref[own] = soft.spread(jnp.where(soft.marked(mine), 0.0, NEG_FILL)).astype(BF16)
        last = (len(picks) - 1) * soft.tokens
        for g in range(soft.kv_heads):
            scores = soft.scores(own, g, marks_ref[own], picks)
            scores = jnp.concatenate([scores[:, :last], scores[:, last:] + fills[...]], 1)
            peak = soft.top(scores)
            at = own * soft.kv_heads + g
            sums_ref[at] = soft.mixed(g, soft.probs(scores, peak), picks)
            peaks_ref[at] = peak


def away_kernel(places, share, at_ref, got_ref, query_ref, home_ref, sums_ref, peaks_ref, marks_ref, *rest):
    pays, rest = rest[: places - 1], rest[places - 1 :]
    given, kept, codes = rest[:PARTS], rest[PARTS], rest[PARTS + 1]
    soft = Soft(places, at_ref, query_ref, got_ref, home_ref, share, codes)
    for own in range(LOOK):
        picks = soft.far(soft.core if own else 1 - soft.core, range(1, places), pays)
        soft.code(own, picks)
        mixed = []
        for g in range(soft.kv_heads):
            at = own * soft.kv_heads + g
            out, _ = soft.added(own, g, marks_ref[own], picks, sums_ref[at], peaks_ref[at])
            mixed.append((out[:, : soft.width] / out[:, soft.width :]).reshape(soft.tokens, share, soft.width))
        mixed = jnp.concatenate(mixed, 1).astype(BF16)
        if own:
            kept[...] = mixed
        else:
            size = soft.tokens // PARTS
            for n in range(PARTS):
                given[n][...] = mixed[n * size : (n + 1) * size]


def body(
    light_query,
    light_keys,
    light_values,
    decay_rate,
    norm_gain,
    soft_query,
    soft_keys,
    soft_values,
    segment_ids,
):
    places = lax.axis_size("head")
    n_all = lax.axis_size("ctx") * places
    members = LOOK * places
    core = lax.rem(lax.axis_index("ctx"), LOOK)
    place = lax.axis_index("head")
    at = jnp.stack([core, place, core * places + place]).astype(jnp.int32)
    tokens, heads, width = light_query.shape
    kv_heads = soft_keys.shape[1]
    per, half, kv_half = heads // places, heads // LOOK, kv_heads // LOOK
    sid_row = segment_ids.reshape(1, tokens)
    even, uneven = [k for k in range(places) if not odd(k)], [k for k in range(places) if odd(k)]

    def partner(value, k):
        pairs = [(i, i - i % members + ((i % members) ^ k)) for i in range(n_all)]
        return lax.ppermute(value, AXES, pairs)

    def across(value):
        return partner(value, places)

    def to_places(values):
        return [values[0]] + [partner(values[k], k) for k in range(1, places)]

    def onward(value, groups):
        step = groups * places
        return lax.ppermute(value, AXES, [(i, i + step) for i in range(n_all - step)])

    def shape(*dims):
        return jax.ShapeDtypeStruct(dims, BF16)

    def room(*dims, dtype=BF16):
        return pltpu.VMEM(dims, dtype)

    def semaphores(count):
        return pltpu.SemaphoreType.DMA((count,))

    pay = shape(2 * kv_half * tokens + TAIL, width)
    pair = shape(LOOK * (pay.shape[0] - TAIL) + TAIL, width)
    given = shape(pay.shape[0] // half + tokens, half, width)
    state = shape(per * width + TAIL, width)
    by_head = shape(heads, tokens, width)
    half_out = shape(tokens, half, width)
    slots = room(places, *state.shape)
    sid_room = room(1, tokens, dtype=jnp.int32)

    def held(value):
        return pltpu.with_memory_space_constraint(value, pltpu.HBM)

    made = call(
        functools.partial(source_kernel, places), "source", 0, 16, [SMEM] + [HBM] * 7,
        [shape(state.shape[0] + TAIL, width)] * places + [by_head] * 2 + [pair, given], [VMEM] * (places + 4),
        [pltpu.SMEM((heads,), F32), sid_room] + [room(tokens, heads, width)] * 2 + [room(tokens, kv_heads, width)] * 2
        + [room(kv_heads, tokens, width), semaphores(5 + 2 * PIECES)],
    )(at, *[held(x) for x in (decay_rate, sid_row, light_keys, light_values, soft_keys, soft_values, soft_query)])
    keys_by_head, values_by_head, own, give = made[places:]
    states = to_places(made[:places])
    got = across(give)
    own = call(pair_kernel, "pair", 0, 8, [SMEM, VMEM, VMEM], pair, VMEM, aliases={2: 0})(at, got, own)
    before = onward(own, LOOK)

    left = call(
        prep_kernel, "prep", 0, 16, [SMEM, VMEM, VMEM, VMEM], shape(heads, tokens, tokens + width), VMEM
    )(decay_rate, sid_row, light_query, keys_by_head)
    mixed = call(
        functools.partial(mix_kernel, places), "mix", 0, 8, [SMEM] + [VMEM] * 2,
        [shape(4, *pay.shape)] + [shape(3 * (pay.shape[0] - TAIL) + TAIL, width)] * (places - 1), [VMEM] * places, after=[left, *[states[k] for k in even[1:]]],
    )(at, own, before)
    home = mixed[0]
    parcels = to_places(mixed)

    ending = call(
        functools.partial(ending_kernel, places, tokens), "ending", 0, 8, [SMEM] * 2 + [VMEM] * places,
        [state] * LOOK, [VMEM] * LOOK, [slots], after=[home],
    )(at, decay_rate, *states)
    ahead = [onward(ending[n], n + 1) for n in range(LOOK)]
    share = half // kv_half
    queries = tokens * share

    def codes(blocks):
        return room(LOOK, blocks * tokens, width)

    def limit(blocks):
        return (blocks * tokens * queries * 14 + 8 * half_out.size) / 2**20 + 8

    sums_like = [
        jax.ShapeDtypeStruct((LOOK * kv_half, queries, 2 * width), F32),
        jax.ShapeDtypeStruct((LOOK * kv_half, queries, width), F32),
    ]
    sums, peaks, marks = call(
        functools.partial(home_kernel, places, share), "home", 0, limit(3), [SMEM] + [VMEM] * 3,
        sums_like + [shape(LOOK, queries, tokens)], [VMEM] * 3, [codes(3), room(queries, tokens, dtype=F32)], after=[ending[0]],
    )(at, got, soft_query, home)
    prefixed = call(
        functools.partial(prefix_kernel, places, tokens), "prefix", 0, 12, [SMEM] * 2 + [VMEM] * (places + LOOK),
        [state] * places, [VMEM] * places, [slots, slots], after=[sums],
    )(at, decay_rate, *ahead, *states)
    entries = to_places(prefixed)

    blocks = 2 * (places - 1)
    part_out = shape(tokens // PARTS, half, width)
    made = call(
        functools.partial(away_kernel, places, share), "away", 30, limit(blocks), [SMEM] + [VMEM] * (5 + places),
        [part_out] * PARTS + [half_out], [VMEM] * (PARTS + 1), [codes(blocks)], after=[prefixed[0]],
    )(at, got, soft_query, home, sums, peaks, marks, *parcels[1:])
    soft_theirs, soft_kept = made[:PARTS], made[PARTS]

    whole = shape(tokens, heads, width)
    known = (at, decay_rate, sid_row, norm_gain, left, values_by_head)
    rooms = [room(half, tokens, width), room(tokens, half, width)]
    made = call(
        functools.partial(first_kernel, places, even), "first", 0, 16,
        [SMEM] * 2 + [VMEM] * 5 + [ANY] * PARTS + [VMEM] * len(even), [whole, whole] + [part_out] * PARTS, [HBM, HBM] + [ANY] * PARTS,
        rooms + [semaphores(1 + PIECES)], aliases={7 + n: 2 + n for n in range(PARTS)},
    )(*known, soft_kept, *soft_theirs, *[entries[k] for k in even])
    soft_got = [across(x) for x in made[2:]]
    return tuple(
        call(
            functools.partial(second_kernel, places, uneven), "second", 15, 16,
            [SMEM] * 2 + [VMEM] * (4 + PARTS) + [HBM] * 2 + [VMEM] * len(uneven), [whole, whole], [HBM, HBM],
            rooms + [semaphores(PIECES + PARTS)], aliases={6 + PARTS: 0, 7 + PARTS: 1},
        )(*known, *soft_got, made[0], made[1], *[entries[k] for k in uneven])
    )


def solution(mesh):
    placed = P(("ctx", "head"), None, None)
    return jax.shard_map(
        body,
        mesh=mesh,
        in_specs=(placed, placed, placed, P(), P(), placed, placed, placed, P(("ctx", "head"))),
        out_specs=(placed, placed),
        check_vma=False,
    )
```
